32 devices in a mesh: lat: 4 (over z), lon: 4 (over x, core), rep: 2 (over y).
Axes of the slice: x: 2, y: 2, z: 4, core: 2. Of those that a mesh axis runs over, the one named last changes fastest.
Arguments:
- latent: bfloat16 [6, 24, 384, 512], P('rep', 'lat', 'lon'), parts along dimension 0, may hold values from -6 to 6
- band_labels: int32 [24], replicated, may hold values from 0 to 5, never falling along the last dimension, each value on 1 to 8 neighbouring positions
- gain_first: float32 [512], replicated, may hold values from 0.1 to 1.9
- qkv_first: bfloat16 [512, 1536], replicated, may hold values from -2 to 2
- proj_first: bfloat16 [512, 512], replicated, may hold values from -1 to 1
- merge_gain: float32 [2048], replicated, may hold values from 0.1 to 1.9
- merge_weight: bfloat16 [2048, 1024], replicated, may hold values from -0.125 to 0.125
- gain_coarse: float32 [1024], replicated, may hold values from 0.1 to 1.9
- qkv_coarse: bfloat16 [1024, 3072], replicated, may hold values from -2 to 2
- proj_coarse: bfloat16 [1024, 1024], replicated, may hold values from -0.75 to 0.75
- split_gain: float32 [1024], replicated, may hold values from 0.1 to 1.9
- split_weight: bfloat16 [1024, 2048], replicated, may hold values from -0.1875 to 0.1875
- gain_last: float32 [512], replicated, may hold values from 0.1 to 1.9
- qkv_last: bfloat16 [512, 1536], replicated, may hold values from -2 to 2
- proj_last: bfloat16 [512, 512], replicated, may hold values from -1 to 1
Outputs:
- forecast_latent: bfloat16 [6, 24, 384, 512], P('rep', 'lat', 'lon'), parts along dimension 0
The draws below stay inside these ranges and needn't reach their ends.
There are 2 independent parts, one for each index of `rep`. The reference program is written for one: setup_inputs(seed, part) draws one part's arguments, and reference() takes and returns one part's arrays. A program takes and returns all parts, laid end to end along the dimension named above; an argument that names none is the same for every part. Nothing has to cross between parts.
Inputs may be any that keep to these rules, and one draw needn't show every extreme that they name: `band_labels`: labels never fall along the rows, and each label covers 1 to 8 consecutive rows.
All inputs are finite; a program needn't handle non-finite values.
Results may differ from the reference program's by a relative error of at most 0.015.
Values may be sent and summed in bfloat16 or wider, within the bound.
No kernel may reach another device: no remote copies, remote signals or barrier semaphores. Data moves between devices by JAX's collectives and lax.ppermute only.
A program may use at most 128 MiB of HBM per device.

```python
import math
import jax
import jax.numpy as jnp
import numpy as np
from jax import lax

D = 512
HEAD_DIM = 64
LEVELS = 3
WIN_ROWS = 6
WIN_COLS = 12
NLAT = 24
NLON = 384
BANDS = 6


def drawn_projection(key, width):
    base = jax.random.normal(key, (width, 3 * width), jnp.float32) * width ** (-0.5)
    return jnp.clip(base, -2.0, 2.0)


def draw_qkv_first(key, part):
    return drawn_projection(jax.random.fold_in(key, 101), D).astype(jnp.bfloat16)


def draw_qkv_coarse(key, part):
    return drawn_projection(jax.random.fold_in(key, 202), 2 * D).astype(jnp.bfloat16)


def draw_qkv_last(key, part):
    return drawn_projection(jax.random.fold_in(key, 303), D).astype(jnp.bfloat16)


def steps_of(own_key, extent, cuts, low, high):
    level = 1.0
    for position, parts in cuts:
        heights = jax.random.uniform(jax.random.fold_in(jax.random.fold_in(own_key, 6), position), (parts,), jnp.float32, low / len(cuts), high / len(cuts))
        level = level * jnp.repeat(jnp.exp(heights), extent[position] // parts).reshape((-1,) + (1,) * (len(extent) - 1 - position))
    return level


def profile(amount, total, most, lean):
    portions = [(1 << 20) // math.isqrt(rank ** lean) + 1 for rank in range(2, amount + 1)]
    rest, counts = total - most - (amount - 1), [1] * (amount - 1)
    while rest > 0:
        free = [i for i in range(amount - 1) if counts[i] < most]
        pool, remaining = sum([portions[i] for i in free]), rest
        for i in free:
            more = min(most - counts[i], max(1, remaining * portions[i] // pool), rest)
            counts[i] = counts[i] + more
            rest = rest - more
    return np.array([most] + counts)


def uneven(stream_key, amount, total, limit, slope):
    if amount == 2:
        one = jax.random.randint(stream_key, (), max(1, total - limit), min(limit, total - 1) + 1)
        return jnp.stack([one, total - one])
    sizes = jnp.asarray(profile(amount, total, limit, slope), jnp.int32)
    couples = (amount - 1) // 2
    giver, taker = sizes[1:1 + 2 * couples:2], sizes[2:2 + 2 * couples:2]
    room = jnp.minimum(giver - 1, limit - taker)
    shifted = jax.random.randint(jax.random.fold_in(stream_key, 1), (couples,), 0, 1 << 20) % (room + 1)
    sizes = sizes.at[1:1 + 2 * couples:2].set(giver - shifted).at[2:2 + 2 * couples:2].set(taker + shifted)
    return sizes[jax.random.permutation(jax.random.fold_in(stream_key, 2), amount)]


def centred(rng, dims, scale, bound, split=(), dtype=jnp.bfloat16):
    values = jax.random.normal(rng, dims, jnp.float32) * scale
    if len(split) > 0:
        values = steps_of(rng, dims, split, -0.22, 0.18) * values
    return jnp.clip(values, min=-bound, max=bound).astype(dtype)


def setup_inputs(seed: int = 0, part: int = 0) -> dict:
    splits = jax.random.split(jax.random.key(seed), 16)
    own_keys = jax.random.split(jax.random.fold_in(splits[15], part), 16)
    latent = centred(own_keys[0], (LEVELS, NLAT, NLON, D), 1.0, 6.0, ((1, 4), (2, 4)))
    band_labels = jnp.searchsorted(jnp.cumsum(uneven(splits[1], BANDS, NLAT, 8, 0)), jnp.arange(NLAT), side="right").astype(jnp.int32)
    gain_first = jnp.clip(1.0 + 0.18 * jax.random.normal(splits[2], (D,), jnp.float32), 0.1, 1.9)
    qkv_first = draw_qkv_first(jax.random.fold_in(splits[15], 71), part)
    proj_first = centred(splits[4], (D, D), (D // 16) ** -0.5, 1.0)
    merge_gain = jnp.clip(1.0 + 0.18 * jax.random.normal(splits[5], (4 * D,), jnp.float32), 0.1, 1.9)
    merge_weight = centred(splits[6], (4 * D, 2 * D), (4 * D) ** -0.5, 0.125)
    gain_coarse = jnp.clip(1.0 + 0.18 * jax.random.normal(splits[7], (2 * D,), jnp.float32), 0.1, 1.9)
    qkv_coarse = draw_qkv_coarse(jax.random.fold_in(splits[15], 71), part)
    proj_coarse = centred(splits[9], (2 * D, 2 * D), (D // 8) ** -0.5, 0.75)
    split_gain = jnp.clip(1.0 + 0.18 * jax.random.normal(splits[10], (2 * D,), jnp.float32), 0.1, 1.9)
    split_weight = centred(splits[11], (2 * D, 4 * D), (2 * D) ** -0.5, 0.1875)
    gain_last = jnp.clip(1.0 + 0.18 * jax.random.normal(splits[12], (D,), jnp.float32), 0.1, 1.9)
    qkv_last = draw_qkv_last(jax.random.fold_in(splits[15], 71), part)
    proj_last = centred(splits[14], (D, D), (D // 16) ** -0.5, 1.0)
    return {"latent": latent, "band_labels": band_labels, "gain_first": gain_first, "qkv_first": qkv_first, "proj_first": proj_first, "merge_gain": merge_gain, "merge_weight": merge_weight, "gain_coarse": gain_coarse, "qkv_coarse": qkv_coarse, "proj_coarse": proj_coarse, "split_gain": split_gain, "split_weight": split_weight, "gain_last": gain_last, "qkv_last": qkv_last, "proj_last": proj_last}


def layer_norm(values, gain):
    wide = values.astype(jnp.float32)
    center = lax.optimization_barrier(jnp.mean(wide, axis=-1, keepdims=True))
    spread = lax.optimization_barrier(jnp.mean(jnp.square(wide - center), axis=-1, keepdims=True))
    return ((wide - center) * lax.rsqrt(spread + 1e-05) * gain).astype(jnp.bfloat16)

def to_windows(field):
    levels, rows, cols, width = field.shape
    count = cols // WIN_COLS
    shaped = field.reshape(levels, rows, count, WIN_COLS, width).transpose(2, 0, 1, 3, 4)
    return shaped.reshape(count, levels * rows * WIN_COLS, width)

def from_windows(blocks, levels, rows):
    count, tokens, width = blocks.shape
    shaped = blocks.reshape(count, levels, rows, WIN_COLS, width).transpose(1, 2, 0, 3, 4)
    return shaped.reshape(levels, rows, count * WIN_COLS, width)

def token_labels(row_labels):
    rows = row_labels.shape[0]
    return jnp.broadcast_to(row_labels[None, :, None], (LEVELS, rows, WIN_COLS)).reshape(-1)

def attend(queries_in, keys_in, qkv_weight, proj_weight, allowed):
    count, query_tokens, width = queries_in.shape
    key_tokens = keys_in.shape[1]
    heads = width // HEAD_DIM
    query = jnp.dot(queries_in.reshape(-1, width), qkv_weight[:, :width], preferred_element_type=jnp.float32)
    query = query.astype(jnp.bfloat16).reshape(count, query_tokens, heads, HEAD_DIM)
    paired = jnp.dot(keys_in.reshape(-1, width), qkv_weight[:, width:], preferred_element_type=jnp.float32)
    paired = paired.astype(jnp.bfloat16).reshape(count, key_tokens, 2, heads, HEAD_DIM)
    scores = jnp.einsum('wqhd,wkhd->whqk', query.astype(jnp.float32), paired[:, :, 0].astype(jnp.float32))
    scores = scores * HEAD_DIM ** (-0.5)
    scores = jnp.where(allowed[None, None], scores, -1e+30)
    highest = lax.optimization_barrier(jnp.max(scores, axis=-1, keepdims=True))
    expo = jnp.exp(scores - highest)
    weights = (expo / lax.optimization_barrier(jnp.sum(expo, axis=-1, keepdims=True))).astype(jnp.bfloat16)
    mixed = jnp.einsum('whqk,wkhd->wqhd', weights.astype(jnp.float32), paired[:, :, 1].astype(jnp.float32))
    mixed = mixed.astype(jnp.bfloat16).reshape(count * query_tokens, width)
    return jnp.dot(mixed, proj_weight, preferred_element_type=jnp.float32).reshape(count, query_tokens, width)

def shifted_block(field, gain, qkv_weight, proj_weight, labels):
    half_rows = WIN_ROWS // 2
    half_cols = WIN_COLS // 2
    rolled = jnp.roll(field, (-half_rows, -half_cols), axis=(1, 2))
    levels, total_rows, total_cols, width = rolled.shape
    bands = rolled.reshape(levels, total_rows // WIN_ROWS, WIN_ROWS, total_cols, width).transpose(1, 0, 2, 3, 4)
    if labels is None:
        band_rows = jnp.zeros((total_rows // WIN_ROWS, WIN_ROWS), jnp.int32)
    else:
        band_rows = jnp.roll(labels, -half_rows).reshape(-1, WIN_ROWS)

    def one_band(inputs):
        band, row_labels = inputs
        tokens = token_labels(row_labels)
        allowed = tokens[:, None] == tokens[None, :]
        normed = to_windows(layer_norm(band, gain))
        branch = from_windows(attend(normed, normed, qkv_weight, proj_weight, allowed), levels, WIN_ROWS)
        return (band.astype(jnp.float32) + branch).astype(jnp.bfloat16)
    finished = lax.map(one_band, (bands, band_rows))
    finished = finished.transpose(1, 0, 2, 3, 4).reshape(levels, total_rows, total_cols, width)
    return jnp.roll(finished, (half_rows, half_cols), axis=(1, 2))

def merge_tokens(field, gain, weight):
    stacked = jnp.concatenate([field[:, 0::2, 0::2], field[:, 1::2, 0::2], field[:, 0::2, 1::2], field[:, 1::2, 1::2]], axis=-1)
    levels, rows, cols, wide = stacked.shape
    normed = layer_norm(stacked, gain).reshape(-1, wide)
    merged = jnp.dot(normed, weight, preferred_element_type=jnp.float32).astype(jnp.bfloat16)
    return merged.reshape(levels, rows, cols, weight.shape[1])

def split_tokens(coarse, gain, weight, skipped):
    levels, rows, cols, wide = coarse.shape
    normed = layer_norm(coarse, gain).reshape(-1, wide)
    spread = jnp.dot(normed, weight, preferred_element_type=jnp.float32)
    width = weight.shape[1] // 4
    placed = spread.reshape(levels, rows, cols, 2, 2, width).transpose(0, 1, 4, 2, 3, 5)
    placed = placed.reshape(levels, 2 * rows, 2 * cols, width)
    return (skipped.astype(jnp.float32) + placed).astype(jnp.bfloat16)

def reference(latent, band_labels, gain_first, qkv_first, proj_first, merge_gain, merge_weight, gain_coarse, qkv_coarse, proj_coarse, split_gain, split_weight, gain_last, qkv_last, proj_last):
    first = shifted_block(latent, gain_first, qkv_first, proj_first, band_labels)
    merged = merge_tokens(first, merge_gain, merge_weight)
    coarse = shifted_block(merged, gain_coarse, qkv_coarse, proj_coarse, None)
    joined = split_tokens(coarse, split_gain, split_weight, first)
    return shifted_block(joined, gain_last, qkv_last, proj_last, band_labels)
```

```python
import functools
import math
import jax
import jax.numpy as jnp
from jax import lax
from jax.experimental import pallas as pl
from jax.experimental.pallas import tpu as pltpu
from jax.sharding import PartitionSpec as P

HEAD_DIM = 64
LEVELS = 3
WIN_ROWS = 6
WIN_COLS = 12
HALF_ROWS = WIN_ROWS // 2
HALF_COLS = WIN_COLS // 2
TOKENS = LEVELS * WIN_ROWS * WIN_COLS
LANES = 128
SCALE = HEAD_DIM**-0.5 * math.log2(math.e)
PARAMS = pltpu.CompilerParams(vmem_limit_bytes=60 * 1024 * 1024)


def norm(wide, gain):
    center = jnp.mean(wide, axis=-1, keepdims=True)
    moved = wide - center
    spread = jnp.mean(jnp.square(moved), axis=-1, keepdims=True)
    return (moved * lax.rsqrt(spread + 1e-05) * gain).astype(jnp.bfloat16)


def rounded(value):
    return value.astype(jnp.bfloat16).astype(jnp.float32)


def attend(x, gain, qkv_ref, proj_ref, bias, qkv_s, mix_s):
    width = x.shape[1]
    normed = norm(x, gain)
    for third in range(3):
        part = jnp.dot(
            normed,
            qkv_ref[:, third * width : (third + 1) * width],
            preferred_element_type=jnp.float32,
        )
        qkv_s[:, third * width : (third + 1) * width] = part.astype(jnp.bfloat16)
    pair = 2 * HEAD_DIM
    low = lax.broadcasted_iota(jnp.int32, (TOKENS, pair), 1) < HEAD_DIM
    ones = jnp.ones((TOKENS, pair), jnp.bfloat16)
    zeros = jnp.zeros((TOKENS, pair), jnp.bfloat16)
    for j in range(width // pair):
        q = qkv_s[:, j * pair : (j + 1) * pair]
        k = qkv_s[:, width + j * pair : width + (j + 1) * pair]
        v = qkv_s[:, 2 * width + j * pair : 2 * width + (j + 1) * pair]
        summed = jnp.concatenate([v, ones], axis=1)
        parts = []
        for keep in (low, ~low):
            s = lax.dot_general(
                q,
                jnp.where(keep, k, zeros),
                (((1,), (1,)), ((), ())),
                preferred_element_type=jnp.float32,
            )
            s = s * SCALE
            if bias is not None:
                s = s + bias
            p = jnp.exp2(s - jnp.max(s, axis=-1, keepdims=True)).astype(jnp.bfloat16)
            r = jnp.dot(p, summed, preferred_element_type=jnp.float32)
            parts.append(r[:, :pair] / r[:, pair:])
        mix_s[:, j * pair : (j + 1) * pair] = jnp.where(low, parts[0], parts[1]).astype(
            jnp.bfloat16
        )
    return rounded(x + jnp.dot(mix_s[...], proj_ref[...], preferred_element_type=jnp.float32))


def row_of(dim):
    t = lax.broadcasted_iota(jnp.int32, (TOKENS, TOKENS), dim)
    group = (t * 43691) >> 19
    return group - WIN_ROWS * ((group * 43691) >> 18)


def make_bias(labels_ref, first_row):
    count = labels_ref.shape[0]
    rows = [row_of(0), row_of(1)]
    marks = [jnp.zeros((TOKENS, TOKENS), jnp.int32) for _ in rows]
    for r in range(WIN_ROWS):
        label = labels_ref[lax.rem(first_row + r + count, count)]
        marks = [jnp.where(row == r, label, mark) for row, mark in zip(rows, marks)]
    return jnp.where(marks[0] == marks[1], 0.0, -1e30)


def strip_of(place, center):
    odd = lax.rem(place, 2) == 1
    is_left = odd if center else jnp.logical_not(odd)
    first_row = WIN_ROWS * place + jnp.where(is_left, HALF_ROWS, -HALF_ROWS)
    return is_left, first_row


def load(win_s, w):
    return jnp.concatenate([win_s[w, c] for c in range(win_s.shape[1])], axis=1)


def store(win_s, w, start, value):
    for c in range(win_s.shape[1]):
        win_s[w, c, start : start + value.shape[0], :] = value[:, c * LANES : (c + 1) * LANES]


def put(win_s, group, start, value):
    at, done = start, 0
    while done < value.shape[0]:
        w, c = divmod(at, WIN_COLS)
        size = min(WIN_COLS - c, value.shape[0] - done)
        store(win_s, w, group * WIN_COLS + c, value[done : done + size])
        at, done = at + size, done + size


def merge_rows(upper, lower, gain, weight):
    levels, cols, wide = upper.shape
    a = upper.reshape(levels * cols, wide)
    b = lower.reshape(levels * cols, wide)
    half = wide // 2
    stacked = jnp.concatenate([a[:, :half], b[:, :half], a[:, half:], b[:, half:]], axis=1)
    out = jnp.dot(norm(stacked, gain), weight, preferred_element_type=jnp.float32)
    return out.astype(jnp.bfloat16).astype(jnp.float32).reshape(levels, cols, wide)


def wide(ref, index):
    return ref[index].astype(jnp.float32)


def first_kernel(
    center,
    half,
    place_ref,
    labels_ref,
    x_ref,
    lon_ref,
    main_ref,
    second_ref,
    gain_ref,
    qkv_ref,
    proj_ref,
    mgain_ref,
    mweight_ref,
    out_ref,
    upper_ref,
    lower_ref,
    win_s,
    qkv_s,
    mix_s,
    bias_s,
):
    is_left, first_row = strip_of(place_ref[0], center)
    cut = x_ref.shape[2] - half - HALF_COLS
    span = half + WIN_COLS

    @pl.when(is_left)
    def _():
        for l in range(LEVELS):
            for r in range(HALF_ROWS):
                own = x_ref[l, HALF_ROWS + r].astype(jnp.float32)
                put(win_s, l * WIN_ROWS + r, 0, own[HALF_COLS : HALF_COLS + span])
                group = l * WIN_ROWS + HALF_ROWS + r
                put(win_s, group, 0, main_ref[l, r].astype(jnp.float32))
                put(win_s, group, cut, second_ref[l, r].astype(jnp.float32))

    @pl.when(jnp.logical_not(is_left))
    def _():
        for l in range(LEVELS):
            for r in range(HALF_ROWS):
                group = l * WIN_ROWS + r
                put(win_s, group, 0, main_ref[l, r].astype(jnp.float32))
                put(win_s, group, cut, second_ref[l, r].astype(jnp.float32))
                group = l * WIN_ROWS + HALF_ROWS + r
                own = x_ref[l, r].astype(jnp.float32)
                put(win_s, group, 0, own[HALF_COLS + half :])
                put(win_s, group, cut, lon_ref[l, r].astype(jnp.float32))

    bias_s[...] = make_bias(labels_ref, first_row)

    def window(w, carry):
        done = attend(
            load(win_s, w), gain_ref[...], qkv_ref, proj_ref, bias_s[...], qkv_s, mix_s
        )
        store(win_s, w, 0, done)
        return carry

    lax.fori_loop(0, win_s.shape[0], window, 0)

    groups = win_s.shape[1]
    for l in range(LEVELS):
        for r in range(WIN_ROWS):
            base = (l * WIN_ROWS + r) * WIN_COLS
            for parity in range(2):
                for c in range(groups):
                    pieces = []
                    for w in range(win_s.shape[0]):
                        skip = HALF_COLS if w == 0 else 0
                        size = HALF_COLS // 2 if w in (0, win_s.shape[0] - 1) else HALF_COLS
                        pieces.append(win_s[w, c, pl.ds(base + skip + parity, size, stride=2), :])
                    at = (parity * groups + c) * LANES
                    out_ref[r, l, :, at : at + LANES] = jnp.concatenate(pieces, axis=0).astype(
                        jnp.bfloat16
                    )
    upper_ref[0] = out_ref[0]
    lower_ref[1] = out_ref[WIN_ROWS - 1]
    upper_ref[1] = merge_rows(
        wide(out_ref, 1), wide(out_ref, 2), mgain_ref[...], mweight_ref[...]
    ).astype(jnp.bfloat16)
    lower_ref[0] = merge_rows(
        wide(out_ref, 3), wide(out_ref, 4), mgain_ref[...], mweight_ref[...]
    ).astype(jnp.bfloat16)


def spread_add(spread, upper, lower):
    width = spread.shape[-1] // 4
    parts = [spread[..., i * width : (i + 1) * width] for i in range(4)]
    top = upper + jnp.concatenate([parts[0], parts[2]], axis=-1)
    bottom = lower + jnp.concatenate([parts[1], parts[3]], axis=-1)
    return top.astype(jnp.bfloat16), bottom.astype(jnp.bfloat16)


def coarse_kernel(
    first_ref,
    upper_ref,
    lower_ref,
    prev_ref,
    next_ref,
    mgain_ref,
    mweight_ref,
    gain_ref,
    qkv_ref,
    proj_ref,
    sgain_ref,
    sweight_ref,
    out_ref,
    to_prev_ref,
    to_next_ref,
    edge_ref,
    win_s,
    spread_s,
    qkv_s,
    mix_s,
):
    levels, cols, width = first_ref.shape[1:]
    rows = [
        wide(prev_ref, 0),
        merge_rows(wide(prev_ref, 1), wide(first_ref, 0), mgain_ref[...], mweight_ref[...]),
        wide(upper_ref, 1),
        wide(lower_ref, 0),
        merge_rows(
            wide(first_ref, WIN_ROWS - 1), wide(next_ref, 0), mgain_ref[...], mweight_ref[...]
        ),
        wide(next_ref, 1),
    ]
    for r in range(WIN_ROWS):
        for l in range(levels):
            for w in range(win_s.shape[0]):
                start = (r * levels + l) * WIN_COLS
                win_s[w, start : start + WIN_COLS, :] = rows[r][l, w * WIN_COLS : (w + 1) * WIN_COLS]

    def window(w, carry):
        done = attend(win_s[w], gain_ref[...], qkv_ref, proj_ref, None, qkv_s, mix_s)
        win_s[w] = done
        spread_s[w] = jnp.dot(
            norm(done, sgain_ref[...]), sweight_ref[...], preferred_element_type=jnp.float32
        )
        return carry

    lax.fori_loop(0, win_s.shape[0], window, 0)

    def gathered(ref, r):
        return jnp.stack(
            [
                jnp.concatenate(
                    [
                        ref[w, (r * levels + l) * WIN_COLS : (r * levels + l + 1) * WIN_COLS, :]
                        for w in range(win_s.shape[0])
                    ],
                    axis=0,
                )
                for l in range(levels)
            ]
        )

    to_prev_ref[0] = gathered(win_s, 0).astype(jnp.bfloat16)
    to_next_ref[1] = gathered(win_s, WIN_ROWS - 1).astype(jnp.bfloat16)
    to_prev_ref[1], out_ref[0] = spread_add(
        gathered(spread_s, 1), wide(prev_ref, 1), wide(first_ref, 0)
    )
    out_ref[1], out_ref[2] = spread_add(
        gathered(spread_s, 2), wide(first_ref, 1), wide(first_ref, 2)
    )
    out_ref[3], out_ref[4] = spread_add(
        gathered(spread_s, 3), wide(first_ref, 3), wide(first_ref, 4)
    )
    out_ref[5], to_next_ref[0] = spread_add(
        gathered(spread_s, 4), wide(first_ref, 5), wide(next_ref, 0)
    )
    for r in range(WIN_ROWS):
        for l in range(levels):
            edge_ref[r, l] = out_ref[r, l].astype(jnp.float32)[-HALF_COLS // 2 :].astype(jnp.bfloat16)


def giver_kernel(
    first_ref, prev_ref, next_ref, sgain_ref, sweight_ref, out_ref, edge_ref
):
    levels, cols, width = first_ref.shape[1:]
    both = jnp.concatenate([wide(prev_ref, 1), wide(next_ref, 0)], axis=0)
    spread = jnp.dot(
        norm(both.reshape(2 * levels * cols, width), sgain_ref[...]),
        sweight_ref[...],
        preferred_element_type=jnp.float32,
    ).reshape(2 * levels, cols, 2 * width)
    out_ref[0] = prev_ref[0]
    out_ref[5] = next_ref[1]
    out_ref[1], out_ref[2] = spread_add(spread[:levels], wide(first_ref, 1), wide(first_ref, 2))
    out_ref[3], out_ref[4] = spread_add(spread[levels:], wide(first_ref, 3), wide(first_ref, 4))
    for r in range(WIN_ROWS):
        for l in range(levels):
            edge_ref[r, l] = out_ref[r, l].astype(jnp.float32)[-HALF_COLS // 2 :].astype(jnp.bfloat16)


def last_kernel(
    center,
    place_ref,
    labels_ref,
    joined_ref,
    edge_ref,
    gain_ref,
    qkv_ref,
    proj_ref,
    own_ref,
    main_ref,
    second_ref,
    win_s,
    qkv_s,
    mix_s,
    bias_s,
    row_s,
):
    is_left, first_row = strip_of(place_ref[0], center)
    groups = win_s.shape[1]
    width = groups * LANES
    extra = edge_ref.shape[2]
    for l in range(LEVELS):
        for r in range(WIN_ROWS):
            base = (l * WIN_ROWS + r) * WIN_COLS
            edge = edge_ref[r, l].astype(jnp.float32)
            joined = joined_ref[r, l].astype(jnp.float32)
            for parity in range(2):
                lanes = slice(parity * width, (parity + 1) * width)
                start = base + parity * HALF_COLS
                store(win_s, 0, start, edge[:, lanes])
                store(win_s, 0, start + extra, joined[: HALF_COLS - extra, lanes])
                for w in range(1, win_s.shape[0]):
                    begin = w * HALF_COLS - extra
                    store(win_s, w, start, joined[begin : begin + HALF_COLS, lanes])

    bias_s[...] = make_bias(labels_ref, first_row)

    def window(w, carry):
        done = attend(
            load(win_s, w), gain_ref[...], qkv_ref, proj_ref, bias_s[...], qkv_s, mix_s
        )
        store(win_s, w, 0, done)
        return carry

    lax.fori_loop(0, win_s.shape[0], window, 0)

    def natural(l, r):
        base = (l * WIN_ROWS + r) * WIN_COLS
        for w in range(win_s.shape[0]):
            for parity in range(2):
                start = base + parity * HALF_COLS
                for c in range(groups):
                    row_s[c, pl.ds(w * WIN_COLS + parity, HALF_COLS, stride=2), :] = win_s[
                        w, c, start : start + HALF_COLS, :
                    ]
        return jnp.concatenate([row_s[c] for c in range(groups)], axis=1)

    cut = main_ref.shape[2]

    def finish(own_row, other_row):
        for l in range(LEVELS):
            for r in range(HALF_ROWS):
                own_ref[l, r] = natural(l, own_row + r).astype(jnp.bfloat16)
                other = natural(l, other_row + r)
                main_ref[l, r] = other[:cut].astype(jnp.bfloat16)
                second_ref[l, r] = other[cut:].astype(jnp.bfloat16)

    @pl.when(is_left)
    def _():
        finish(0, HALF_ROWS)

    @pl.when(jnp.logical_not(is_left))
    def _():
        finish(HALF_ROWS, 0)


def bf16(*shape):
    return jax.ShapeDtypeStruct(shape, jnp.bfloat16)


SMEM = pl.BlockSpec(memory_space=pltpu.SMEM)
VMEM = pl.BlockSpec(memory_space=pltpu.VMEM)


def call_first(center, half, place, labels, x, lon, main, second, gain, qkv, proj, mgain, mweight):
    width = x.shape[-1]
    cols = half // 2
    count = half // WIN_COLS + 1
    paired = (LEVELS, cols, 2 * width)
    return pl.pallas_call(
        functools.partial(first_kernel, center, half),
        out_shape=(bf16(WIN_ROWS, *paired), bf16(2, *paired), bf16(2, *paired)),
        in_specs=[SMEM, SMEM] + [VMEM] * 9,
        out_specs=(VMEM, VMEM, VMEM),
        scratch_shapes=[
            pltpu.VMEM((count, width // LANES, TOKENS, LANES), jnp.float32),
            pltpu.VMEM((TOKENS, 3 * width), jnp.bfloat16),
            pltpu.VMEM((TOKENS, width), jnp.bfloat16),
            pltpu.VMEM((TOKENS, TOKENS), jnp.float32),
        ],
        compiler_params=PARAMS,
    )(place, labels, x, lon, main, second, gain, qkv, proj, mgain, mweight)


def call_coarse(first, upper, lower, prev, following, mgain, mweight, gain, qkv, proj, sgain, sweight):
    rows, levels, cols, width = first.shape
    count = cols // WIN_COLS
    paired = (levels, cols, width)
    return pl.pallas_call(
        coarse_kernel,
        out_shape=(
            bf16(rows, *paired),
            bf16(2, *paired),
            bf16(2, *paired),
            bf16(rows, levels, HALF_COLS // 2, width),
        ),
        in_specs=[VMEM] * 12,
        out_specs=(VMEM,) * 4,
        scratch_shapes=[
            pltpu.VMEM((count, TOKENS, width), jnp.float32),
            pltpu.VMEM((count, TOKENS, 2 * width), jnp.float32),
            pltpu.VMEM((TOKENS, 3 * width), jnp.bfloat16),
            pltpu.VMEM((TOKENS, width), jnp.bfloat16),
        ],
        compiler_params=PARAMS,
    )(first, upper, lower, prev, following, mgain, mweight, gain, qkv, proj, sgain, sweight)


def call_giver(first, prev, following, sgain, sweight):
    rows, levels, cols, width = first.shape
    return pl.pallas_call(
        giver_kernel,
        out_shape=(bf16(*first.shape), bf16(rows, levels, HALF_COLS // 2, width)),
        in_specs=[VMEM] * 5,
        out_specs=(VMEM,) * 2,
        compiler_params=PARAMS,
    )(first, prev, following, sgain, sweight)


def call_last(center, place, labels, joined, edge, gain, qkv, proj):
    rows, levels, cols, wide_width = joined.shape
    width = wide_width // 2
    half = 2 * cols
    count = half // WIN_COLS
    return pl.pallas_call(
        functools.partial(last_kernel, center),
        out_shape=(
            bf16(levels, HALF_ROWS, half, width),
            bf16(levels, HALF_ROWS, half - HALF_COLS, width),
            bf16(levels, HALF_ROWS, HALF_COLS, width),
        ),
        in_specs=[SMEM, SMEM] + [VMEM] * 5,
        out_specs=(VMEM,) * 3,
        scratch_shapes=[
            pltpu.VMEM((count, width // LANES, TOKENS, LANES), jnp.float32),
            pltpu.VMEM((TOKENS, 3 * width), jnp.bfloat16),
            pltpu.VMEM((TOKENS, width), jnp.bfloat16),
            pltpu.VMEM((TOKENS, TOKENS), jnp.float32),
            pltpu.VMEM((width // LANES, half, LANES), jnp.float32),
        ],
        compiler_params=PARAMS,
    )(place, labels, joined, edge, gain, qkv, proj)


def send(value, move):
    lats, lons = lax.axis_size("lat"), lax.axis_size("lon")
    pairs = []
    for lat in range(lats):
        for lon in range(lons):
            up, over = move(lat % 2 == 1)
            target = ((lat + up) % lats) * lons + (lon + over) % lons
            pairs.append((lat * lons + lon, target))
    return lax.ppermute(value, ("lat", "lon"), pairs)


def body(
    latent,
    band_labels,
    gain_first,
    qkv_first,
    proj_first,
    merge_gain,
    merge_weight,
    gain_coarse,
    qkv_coarse,
    proj_coarse,
    split_gain,
    split_weight,
    gain_last,
    qkv_last,
    proj_last,
):
    place = lax.axis_index("lat")
    odd = place % 2 == 1
    place = place.reshape(1).astype(jnp.int32)
    cols = latent.shape[2]
    half = cols // 2
    edge = HALF_COLS + half
    cut = cols - edge
    flat = lambda gain: gain.reshape(1, -1)

    for_prev = latent[:, :HALF_ROWS]
    for_next = latent[:, HALF_ROWS:]
    prev_main = for_prev[:, :, HALF_COLS : HALF_COLS + cut]
    prev_second = for_prev[:, :, HALF_COLS + cut : edge + WIN_COLS]
    next_main = for_next[:, :, edge:]
    next_second = for_next[:, :, : WIN_COLS + HALF_COLS]
    lon = send(for_prev[:, :, : WIN_COLS + HALF_COLS], lambda is_odd: (0, -1))
    x_main = send(jnp.where(odd, prev_main, next_main), lambda is_odd: (-1, 0) if is_odd else (1, 0))
    x_second = send(
        jnp.where(odd, prev_second, next_second), lambda is_odd: (-1, 0) if is_odd else (1, -1)
    )
    c_main = send(jnp.where(odd, next_main, prev_main), lambda is_odd: (1, 0) if is_odd else (-1, 0))
    c_second = send(
        jnp.where(odd, next_second, prev_second), lambda is_odd: (1, -1) if is_odd else (-1, 0)
    )

    weights = (flat(gain_first), qkv_first, proj_first, flat(merge_gain), merge_weight)
    first_x, upper_x, lower_x = call_first(
        False, half, place, band_labels, latent, lon, x_main, x_second, *weights
    )
    from_next = send(upper_x, lambda is_odd: (-1, 0))
    from_prev = send(lower_x, lambda is_odd: (1, 0))
    first_c, upper_c, lower_c = call_first(
        True, half, place, band_labels, latent, lon, c_main, c_second, *weights
    )
    joined_c, to_prev, to_next, edge_c = call_coarse(
        first_c,
        upper_c,
        lower_c,
        from_prev,
        from_next,
        flat(merge_gain),
        merge_weight,
        flat(gain_coarse),
        qkv_coarse,
        proj_coarse,
        flat(split_gain),
        split_weight,
    )
    edge_c = send(edge_c, lambda is_odd: (1, 0) if is_odd else (-1, 1))
    back_next = send(to_prev, lambda is_odd: (-1, 0))
    back_prev = send(to_next, lambda is_odd: (1, 0))
    weights = (flat(gain_last), qkv_last, proj_last)
    own_c, main_c, second_c = call_last(True, place, band_labels, joined_c, edge_c, *weights)
    main_c = send(main_c, lambda is_odd: (1, 0) if is_odd else (-1, 0))
    second_c = send(second_c, lambda is_odd: (1, 0) if is_odd else (-1, 1))
    joined_x, edge_x = call_giver(first_x, back_prev, back_next, flat(split_gain), split_weight)
    edge_x = send(edge_x, lambda is_odd: (-1, 1) if is_odd else (1, 0))
    own_x, main_x, second_x = call_last(False, place, band_labels, joined_x, edge_x, *weights)
    main_x = send(main_x, lambda is_odd: (-1, 0) if is_odd else (1, 0))
    second_x = send(second_x, lambda is_odd: (-1, 1) if is_odd else (1, 0))

    own_left = jnp.where(odd, own_c, own_x)
    own_right = jnp.where(odd, own_x, own_c)
    lon_back = send(own_right[:, :, cut:], lambda is_odd: (0, 1))
    left_main, left_second = jnp.where(odd, main_x, main_c), jnp.where(odd, second_x, second_c)
    right_main, right_second = jnp.where(odd, main_c, main_x), jnp.where(odd, second_c, second_x)
    top = jnp.concatenate([lon_back, left_main, left_second, own_right[:, :, :cut]], axis=2)
    bottom = jnp.concatenate([right_second, own_left, right_main], axis=2)
    return jnp.concatenate([top, bottom], axis=1)


def solution(mesh):
    return jax.shard_map(
        body,
        mesh=mesh,
        in_specs=(P("rep", "lat", "lon", None),) + (P(),) * 14,
        out_specs=P("rep", "lat", "lon", None),
        check_vma=False,
    )
```

```python
import functools
import math
import jax
import jax.numpy as jnp
from jax import lax
from jax.experimental import pallas as pl
from jax.experimental.pallas import tpu as pltpu
from jax.sharding import PartitionSpec as P

HEAD_DIM = 64
LEVELS = 3
WIN_ROWS = 6
WIN_COLS = 12
HALF_ROWS = WIN_ROWS // 2
HALF_COLS = WIN_COLS // 2
TOKENS = LEVELS * WIN_ROWS * WIN_COLS
LANES = 128
AT_ONCE = 2
SCALE = HEAD_DIM**-0.5 * math.log2(math.e)
PARAMS = pltpu.CompilerParams(vmem_limit_bytes=28 * 1024 * 1024)


def norm(wide, gain):
    center = jnp.mean(wide, axis=-1, keepdims=True)
    moved = wide - center
    spread = jnp.mean(jnp.square(moved), axis=-1, keepdims=True)
    return (moved * lax.rsqrt(spread + 1e-05) * gain).astype(jnp.bfloat16)


def rounded(value):
    return value.astype(jnp.bfloat16).astype(jnp.float32)


def attend(windows, gain, qkv_ref, proj_ref, bias, qkv_s, mix_s):
    width = windows[0].shape[1]
    pair = 2 * HEAD_DIM
    for i, x in enumerate(windows):
        normed = norm(x, gain)
        for third in range(3):
            lanes = slice(third * width, (third + 1) * width)
            part = jnp.dot(normed, qkv_ref[:, lanes], preferred_element_type=jnp.float32)
            qkv_s[i, :, lanes] = part.astype(jnp.bfloat16)
    low = lax.broadcasted_iota(jnp.int32, (TOKENS, pair), 1) < HEAD_DIM
    ones = jnp.ones((TOKENS, pair), jnp.bfloat16)
    zeros = jnp.zeros((TOKENS, pair), jnp.bfloat16)
    steps = [
        (i, j, keep)
        for j in range(width // pair)
        for i in range(len(windows))
        for keep in (low, ~low)
    ]

    def scored(step):
        i, j, keep = step
        q = qkv_s[i, :, j * pair : (j + 1) * pair]
        k = qkv_s[i, :, width + j * pair : width + (j + 1) * pair]
        return lax.dot_general(
            q,
            jnp.where(keep, k, zeros),
            (((1,), (1,)), ((), ())),
            preferred_element_type=jnp.float32,
        )

    first = None
    ahead = scored(steps[0])
    for n, (i, j, keep) in enumerate(steps):
        s = ahead * SCALE
        if n + 1 < len(steps):
            ahead = scored(steps[n + 1])
        if bias is not None:
            s = s + bias
        p = jnp.exp2(s - jnp.max(s, axis=-1, keepdims=True)).astype(jnp.bfloat16)
        v = qkv_s[i, :, 2 * width + j * pair : 2 * width + (j + 1) * pair]
        r = jnp.dot(p, jnp.concatenate([v, ones], axis=1), preferred_element_type=jnp.float32)
        if n % 2 == 0:
            first = r
        else:
            mixed = jnp.where(low, first[:, :pair], r[:, :pair])
            total = jnp.where(low, first[:, pair:], r[:, pair:])
            mix_s[i, :, j * pair : (j + 1) * pair] = (mixed / total).astype(jnp.bfloat16)
    return [
        rounded(x + jnp.dot(mix_s[i], proj_ref[...], preferred_element_type=jnp.float32))
        for i, x in enumerate(windows)
    ]


def row_of(dim):
    t = lax.broadcasted_iota(jnp.int32, (TOKENS, TOKENS), dim)
    group = (t * 43691) >> 19
    return group - WIN_ROWS * ((group * 43691) >> 18)


def make_bias(labels_ref, first_row):
    count = labels_ref.shape[0]
    rows = [row_of(0), row_of(1)]
    marks = [jnp.zeros((TOKENS, TOKENS), jnp.int32) for _ in rows]
    for r in range(WIN_ROWS):
        label = labels_ref[lax.rem(first_row + r + count, count)]
        marks = [jnp.where(row == r, label, mark) for row, mark in zip(rows, marks)]
    return jnp.where(marks[0] == marks[1], 0.0, -1e30)


def strip_of(place, center):
    odd = lax.rem(place, 2) == 1
    is_left = odd if center else jnp.logical_not(odd)
    first_row = WIN_ROWS * place + jnp.where(is_left, HALF_ROWS, -HALF_ROWS)
    return is_left, first_row


def load(win_s, w):
    return jnp.concatenate([win_s[w, c] for c in range(win_s.shape[1])], axis=1)


def store(win_s, w, start, value):
    for c in range(win_s.shape[1]):
        win_s[w, c, start : start + value.shape[0], :] = value[:, c * LANES : (c + 1) * LANES]


def attend_all(win_s, gain_ref, qkv_ref, proj_ref, bias_s, qkv_s, mix_s):
    count = win_s.shape[0]

    def some(start, size):
        windows = [load(win_s, start + i) for i in range(size)]
        done = attend(windows, gain_ref[...], qkv_ref, proj_ref, bias_s[...], qkv_s, mix_s)
        for i in range(size):
            store(win_s, start + i, 0, done[i])

    def step(n, carry):
        some(n * AT_ONCE, AT_ONCE)
        return carry

    lax.fori_loop(0, count // AT_ONCE, step, 0)
    if count % AT_ONCE:
        some(count - count % AT_ONCE, count % AT_ONCE)


def put(win_s, group, start, value):
    at, done = start, 0
    while done < value.shape[0]:
        w, c = divmod(at, WIN_COLS)
        size = min(WIN_COLS - c, value.shape[0] - done)
        store(win_s, w, group * WIN_COLS + c, value[done : done + size])
        at, done = at + size, done + size


def merge_rows(upper, lower, gain, weight):
    levels, cols, wide = upper.shape
    a = upper.reshape(levels * cols, wide)
    b = lower.reshape(levels * cols, wide)
    half = wide // 2
    stacked = jnp.concatenate([a[:, :half], b[:, :half], a[:, half:], b[:, half:]], axis=1)
    out = jnp.dot(norm(stacked, gain), weight, preferred_element_type=jnp.float32)
    return out.astype(jnp.bfloat16).astype(jnp.float32).reshape(levels, cols, wide)


def wide(ref, index):
    return ref[index].astype(jnp.float32)


def first_kernel(
    center,
    half,
    place_ref,
    labels_ref,
    x_ref,
    lon_ref,
    main_ref,
    second_ref,
    gain_ref,
    qkv_ref,
    proj_ref,
    mgain_ref,
    mweight_ref,
    out_ref,
    upper_ref,
    lower_ref,
    win_s,
    qkv_s,
    mix_s,
    bias_s,
):
    is_left, first_row = strip_of(place_ref[0], center)
    cut = x_ref.shape[2] - half - HALF_COLS
    span = half + WIN_COLS

    @pl.when(is_left)
    def _():
        for l in range(LEVELS):
            for r in range(HALF_ROWS):
                own = x_ref[l, HALF_ROWS + r].astype(jnp.float32)
                put(win_s, l * WIN_ROWS + r, 0, own[HALF_COLS : HALF_COLS + span])
                group = l * WIN_ROWS + HALF_ROWS + r
                put(win_s, group, 0, main_ref[l, r].astype(jnp.float32))
                put(win_s, group, cut, second_ref[l, r].astype(jnp.float32))

    @pl.when(jnp.logical_not(is_left))
    def _():
        for l in range(LEVELS):
            for r in range(HALF_ROWS):
                group = l * WIN_ROWS + r
                put(win_s, group, 0, main_ref[l, r].astype(jnp.float32))
                put(win_s, group, cut, second_ref[l, r].astype(jnp.float32))
                group = l * WIN_ROWS + HALF_ROWS + r
                own = x_ref[l, r].astype(jnp.float32)
                put(win_s, group, 0, own[HALF_COLS + half :])
                put(win_s, group, cut, lon_ref[l, r].astype(jnp.float32))

    bias_s[...] = make_bias(labels_ref, first_row)

    attend_all(win_s, gain_ref, qkv_ref, proj_ref, bias_s, qkv_s, mix_s)

    groups = win_s.shape[1]
    for l in range(LEVELS):
        for r in range(WIN_ROWS):
            base = (l * WIN_ROWS + r) * WIN_COLS
            for parity in range(2):
                for c in range(groups):
                    pieces = []
                    for w in range(win_s.shape[0]):
                        skip = HALF_COLS if w == 0 else 0
                        size = HALF_COLS // 2 if w in (0, win_s.shape[0] - 1) else HALF_COLS
                        pieces.append(win_s[w, c, pl.ds(base + skip + parity, size, stride=2), :])
                    at = (parity * groups + c) * LANES
                    out_ref[r, l, :, at : at + LANES] = jnp.concatenate(pieces, axis=0).astype(
                        jnp.bfloat16
                    )
    upper_ref[0] = out_ref[0]
    lower_ref[1] = out_ref[WIN_ROWS - 1]
    upper_ref[1] = merge_rows(
        wide(out_ref, 1), wide(out_ref, 2), mgain_ref[...], mweight_ref[...]
    ).astype(jnp.bfloat16)
    lower_ref[0] = merge_rows(
        wide(out_ref, 3), wide(out_ref, 4), mgain_ref[...], mweight_ref[...]
    ).astype(jnp.bfloat16)


def spread_add(spread, upper, lower):
    width = spread.shape[-1] // 4
    parts = [spread[..., i * width : (i + 1) * width] for i in range(4)]
    top = upper + jnp.concatenate([parts[0], parts[2]], axis=-1)
    bottom = lower + jnp.concatenate([parts[1], parts[3]], axis=-1)
    return top.astype(jnp.bfloat16), bottom.astype(jnp.bfloat16)


def coarse_kernel(
    first_ref,
    upper_ref,
    lower_ref,
    prev_ref,
    next_ref,
    mgain_ref,
    mweight_ref,
    gain_ref,
    qkv_ref,
    proj_ref,
    sgain_ref,
    sweight_ref,
    out_ref,
    to_prev_ref,
    to_next_ref,
    edge_ref,
    win_s,
    spread_s,
    qkv_s,
    mix_s,
):
    levels, cols, width = first_ref.shape[1:]
    rows = [
        wide(prev_ref, 0),
        merge_rows(wide(prev_ref, 1), wide(first_ref, 0), mgain_ref[...], mweight_ref[...]),
        wide(upper_ref, 1),
        wide(lower_ref, 0),
        merge_rows(
            wide(first_ref, WIN_ROWS - 1), wide(next_ref, 0), mgain_ref[...], mweight_ref[...]
        ),
        wide(next_ref, 1),
    ]
    for r in range(WIN_ROWS):
        for l in range(levels):
            for w in range(win_s.shape[0]):
                start = (r * levels + l) * WIN_COLS
                win_s[w, start : start + WIN_COLS, :] = rows[r][l, w * WIN_COLS : (w + 1) * WIN_COLS]

    count = qkv_s.shape[0]

    def step(n, carry):
        windows = [win_s[n * count + i] for i in range(count)]
        done = attend(windows, gain_ref[...], qkv_ref, proj_ref, None, qkv_s, mix_s)
        for i in range(count):
            win_s[n * count + i] = done[i]
            spread_s[n * count + i] = jnp.dot(
                norm(done[i], sgain_ref[...]), sweight_ref[...], preferred_element_type=jnp.float32
            )
        return carry

    lax.fori_loop(0, win_s.shape[0] // count, step, 0)

    def gathered(ref, r):
        return jnp.stack(
            [
                jnp.concatenate(
                    [
                        ref[w, (r * levels + l) * WIN_COLS : (r * levels + l + 1) * WIN_COLS, :]
                        for w in range(win_s.shape[0])
                    ],
                    axis=0,
                )
                for l in range(levels)
            ]
        )

    to_prev_ref[0] = gathered(win_s, 0).astype(jnp.bfloat16)
    to_next_ref[1] = gathered(win_s, WIN_ROWS - 1).astype(jnp.bfloat16)
    to_prev_ref[1], out_ref[0] = spread_add(
        gathered(spread_s, 1), wide(prev_ref, 1), wide(first_ref, 0)
    )
    out_ref[1], out_ref[2] = spread_add(
        gathered(spread_s, 2), wide(first_ref, 1), wide(first_ref, 2)
    )
    out_ref[3], out_ref[4] = spread_add(
        gathered(spread_s, 3), wide(first_ref, 3), wide(first_ref, 4)
    )
    out_ref[5], to_next_ref[0] = spread_add(
        gathered(spread_s, 4), wide(first_ref, 5), wide(next_ref, 0)
    )
    for r in range(WIN_ROWS):
        for l in range(levels):
            edge_ref[r, l] = out_ref[r, l].astype(jnp.float32)[-HALF_COLS // 2 :].astype(jnp.bfloat16)


def giver_kernel(
    first_ref, prev_ref, next_ref, sgain_ref, sweight_ref, out_ref, edge_ref
):
    levels, cols, width = first_ref.shape[1:]
    both = jnp.concatenate([wide(prev_ref, 1), wide(next_ref, 0)], axis=0)
    spread = jnp.dot(
        norm(both.reshape(2 * levels * cols, width), sgain_ref[...]),
        sweight_ref[...],
        preferred_element_type=jnp.float32,
    ).reshape(2 * levels, cols, 2 * width)
    out_ref[0] = prev_ref[0]
    out_ref[5] = next_ref[1]
    out_ref[1], out_ref[2] = spread_add(spread[:levels], wide(first_ref, 1), wide(first_ref, 2))
    out_ref[3], out_ref[4] = spread_add(spread[levels:], wide(first_ref, 3), wide(first_ref, 4))
    for r in range(WIN_ROWS):
        for l in range(levels):
            edge_ref[r, l] = out_ref[r, l].astype(jnp.float32)[-HALF_COLS // 2 :].astype(jnp.bfloat16)


def last_kernel(
    center,
    place_ref,
    labels_ref,
    joined_ref,
    edge_ref,
    gain_ref,
    qkv_ref,
    proj_ref,
    own_ref,
    main_ref,
    second_ref,
    win_s,
    qkv_s,
    mix_s,
    bias_s,
    row_s,
):
    is_left, first_row = strip_of(place_ref[0], center)
    groups = win_s.shape[1]
    width = groups * LANES
    extra = edge_ref.shape[2]
    for l in range(LEVELS):
        for r in range(WIN_ROWS):
            base = (l * WIN_ROWS + r) * WIN_COLS
            edge = edge_ref[r, l].astype(jnp.float32)
            joined = joined_ref[r, l].astype(jnp.float32)
            for parity in range(2):
                lanes = slice(parity * width, (parity + 1) * width)
                start = base + parity * HALF_COLS
                store(win_s, 0, start, edge[:, lanes])
                store(win_s, 0, start + extra, joined[: HALF_COLS - extra, lanes])
                for w in range(1, win_s.shape[0]):
                    begin = w * HALF_COLS - extra
                    store(win_s, w, start, joined[begin : begin + HALF_COLS, lanes])

    bias_s[...] = make_bias(labels_ref, first_row)

    attend_all(win_s, gain_ref, qkv_ref, proj_ref, bias_s, qkv_s, mix_s)

    def natural(l, r):
        base = (l * WIN_ROWS + r) * WIN_COLS
        for w in range(win_s.shape[0]):
            for parity in range(2):
                start = base + parity * HALF_COLS
                for c in range(groups):
                    row_s[c, pl.ds(w * WIN_COLS + parity, HALF_COLS, stride=2), :] = win_s[
                        w, c, start : start + HALF_COLS, :
                    ]
        return jnp.concatenate([row_s[c] for c in range(groups)], axis=1)

    cut = main_ref.shape[2]

    def finish(own_row, other_row):
        for l in range(LEVELS):
            for r in range(HALF_ROWS):
                own_ref[l, r] = natural(l, own_row + r).astype(jnp.bfloat16)
                other = natural(l, other_row + r)
                main_ref[l, r] = other[:cut].astype(jnp.bfloat16)
                second_ref[l, r] = other[cut:].astype(jnp.bfloat16)

    @pl.when(is_left)
    def _():
        finish(0, HALF_ROWS)

    @pl.when(jnp.logical_not(is_left))
    def _():
        finish(HALF_ROWS, 0)


def bf16(*shape):
    return jax.ShapeDtypeStruct(shape, jnp.bfloat16)


def lasting(micros):
    return pl.CostEstimate(flops=0, bytes_accessed=int(micros * 3.69e6), transcendentals=0)


SMEM = pl.BlockSpec(memory_space=pltpu.SMEM)
VMEM = pl.BlockSpec(memory_space=pltpu.VMEM)


def call_first(center, half, place, labels, x, lon, main, second, gain, qkv, proj, mgain, mweight):
    width = x.shape[-1]
    cols = half // 2
    count = half // WIN_COLS + 1
    paired = (LEVELS, cols, 2 * width)
    return pl.pallas_call(
        functools.partial(first_kernel, center, half),
        out_shape=(bf16(WIN_ROWS, *paired), bf16(2, *paired), bf16(2, *paired)),
        in_specs=[SMEM, SMEM] + [VMEM] * 9,
        out_specs=(VMEM, VMEM, VMEM),
        scratch_shapes=[
            pltpu.VMEM((count, width // LANES, TOKENS, LANES), jnp.float32),
            pltpu.VMEM((AT_ONCE, TOKENS, 3 * width), jnp.bfloat16),
            pltpu.VMEM((AT_ONCE, TOKENS, width), jnp.bfloat16),
            pltpu.VMEM((TOKENS, TOKENS), jnp.float32),
        ],
        cost_estimate=lasting(13),
        compiler_params=PARAMS,
    )(place, labels, x, lon, main, second, gain, qkv, proj, mgain, mweight)


def call_coarse(first, upper, lower, prev, following, mgain, mweight, gain, qkv, proj, sgain, sweight):
    rows, levels, cols, width = first.shape
    count = cols // WIN_COLS
    paired = (levels, cols, width)
    return pl.pallas_call(
        coarse_kernel,
        out_shape=(
            bf16(rows, *paired),
            bf16(2, *paired),
            bf16(2, *paired),
            bf16(rows, levels, HALF_COLS // 2, width),
        ),
        in_specs=[VMEM] * 12,
        out_specs=(VMEM,) * 4,
        scratch_shapes=[
            pltpu.VMEM((count, TOKENS, width), jnp.float32),
            pltpu.VMEM((count, TOKENS, 2 * width), jnp.float32),
            pltpu.VMEM((math.gcd(count, AT_ONCE), TOKENS, 3 * width), jnp.bfloat16),
            pltpu.VMEM((math.gcd(count, AT_ONCE), TOKENS, width), jnp.bfloat16),
        ],
        cost_estimate=lasting(18),
        compiler_params=PARAMS,
    )(first, upper, lower, prev, following, mgain, mweight, gain, qkv, proj, sgain, sweight)


def call_giver(first, prev, following, sgain, sweight):
    rows, levels, cols, width = first.shape
    return pl.pallas_call(
        giver_kernel,
        out_shape=(bf16(*first.shape), bf16(rows, levels, HALF_COLS // 2, width)),
        in_specs=[VMEM] * 5,
        out_specs=(VMEM,) * 2,
        cost_estimate=lasting(4),
        compiler_params=PARAMS,
    )(first, prev, following, sgain, sweight)


def call_last(center, place, labels, joined, edge, gain, qkv, proj):
    rows, levels, cols, wide_width = joined.shape
    width = wide_width // 2
    half = 2 * cols
    count = half // WIN_COLS
    return pl.pallas_call(
        functools.partial(last_kernel, center),
        out_shape=(
            bf16(levels, HALF_ROWS, half, width),
            bf16(levels, HALF_ROWS, half - HALF_COLS, width),
            bf16(levels, HALF_ROWS, HALF_COLS, width),
        ),
        in_specs=[SMEM, SMEM] + [VMEM] * 5,
        out_specs=(VMEM,) * 3,
        scratch_shapes=[
            pltpu.VMEM((count, width // LANES, TOKENS, LANES), jnp.float32),
            pltpu.VMEM((AT_ONCE, TOKENS, 3 * width), jnp.bfloat16),
            pltpu.VMEM((AT_ONCE, TOKENS, width), jnp.bfloat16),
            pltpu.VMEM((TOKENS, TOKENS), jnp.float32),
            pltpu.VMEM((width // LANES, half, LANES), jnp.float32),
        ],
        cost_estimate=lasting(9),
        compiler_params=PARAMS,
    )(place, labels, joined, edge, gain, qkv, proj)


def send(value, move):
    lats, lons = lax.axis_size("lat"), lax.axis_size("lon")
    pairs = []
    for lat in range(lats):
        for lon in range(lons):
            up, over = move(lat % 2 == 1)
            target = ((lat + up) % lats) * lons + (lon + over) % lons
            pairs.append((lat * lons + lon, target))
    return lax.ppermute(value, ("lat", "lon"), pairs)


def body(
    latent,
    band_labels,
    gain_first,
    qkv_first,
    proj_first,
    merge_gain,
    merge_weight,
    gain_coarse,
    qkv_coarse,
    proj_coarse,
    split_gain,
    split_weight,
    gain_last,
    qkv_last,
    proj_last,
):
    place = lax.axis_index("lat")
    odd = place % 2 == 1
    place = place.reshape(1).astype(jnp.int32)
    cols = latent.shape[2]
    half = cols // 2
    edge = HALF_COLS + half
    cut = cols - edge
    flat = lambda gain: gain.reshape(1, -1)

    for_prev = latent[:, :HALF_ROWS]
    for_next = latent[:, HALF_ROWS:]
    prev_main = for_prev[:, :, HALF_COLS : HALF_COLS + cut]
    prev_second = for_prev[:, :, HALF_COLS + cut : edge + WIN_COLS]
    next_main = for_next[:, :, edge:]
    next_second = for_next[:, :, : WIN_COLS + HALF_COLS]
    lon = send(for_prev[:, :, : WIN_COLS + HALF_COLS], lambda is_odd: (0, -1))
    x_main = send(jnp.where(odd, prev_main, next_main), lambda is_odd: (-1, 0) if is_odd else (1, 0))
    x_second = send(
        jnp.where(odd, prev_second, next_second), lambda is_odd: (-1, 0) if is_odd else (1, -1)
    )
    c_main = send(jnp.where(odd, next_main, prev_main), lambda is_odd: (1, 0) if is_odd else (-1, 0))
    c_second = send(
        jnp.where(odd, next_second, prev_second), lambda is_odd: (1, -1) if is_odd else (-1, 0)
    )

    x_main, c_second = lax.optimization_barrier((x_main, c_second))
    weights = (flat(gain_first), qkv_first, proj_first, flat(merge_gain), merge_weight)
    first_x, upper_x, lower_x = call_first(
        False, half, place, band_labels, latent, lon, x_main, x_second, *weights
    )
    from_next = send(upper_x, lambda is_odd: (-1, 0))
    from_prev = send(lower_x, lambda is_odd: (1, 0))
    first_c, upper_c, lower_c = call_first(
        True, half, place, band_labels, latent, lon, c_main, c_second, *weights
    )
    joined_c, to_prev, to_next, edge_c = call_coarse(
        first_c,
        upper_c,
        lower_c,
        from_prev,
        from_next,
        flat(merge_gain),
        merge_weight,
        flat(gain_coarse),
        qkv_coarse,
        proj_coarse,
        flat(split_gain),
        split_weight,
    )
    edge_c = send(edge_c, lambda is_odd: (1, 0) if is_odd else (-1, 1))
    back_next = send(to_prev, lambda is_odd: (-1, 0))
    back_prev = send(to_next, lambda is_odd: (1, 0))
    weights = (flat(gain_last), qkv_last, proj_last)
    own_c, main_c, second_c = call_last(True, place, band_labels, joined_c, edge_c, *weights)
    main_c = send(main_c, lambda is_odd: (1, 0) if is_odd else (-1, 0))
    second_c = send(second_c, lambda is_odd: (1, 0) if is_odd else (-1, 1))
    own_c, first_x = lax.optimization_barrier((own_c, first_x))
    joined_x, edge_x = call_giver(first_x, back_prev, back_next, flat(split_gain), split_weight)
    edge_x = send(edge_x, lambda is_odd: (-1, 1) if is_odd else (1, 0))
    own_x, main_x, second_x = call_last(False, place, band_labels, joined_x, edge_x, *weights)
    main_x = send(main_x, lambda is_odd: (-1, 0) if is_odd else (1, 0))
    second_x = send(second_x, lambda is_odd: (-1, 1) if is_odd else (1, 0))

    own_left = jnp.where(odd, own_c, own_x)
    own_right = jnp.where(odd, own_x, own_c)
    lon_back = send(own_right[:, :, cut:], lambda is_odd: (0, 1))
    left_main, left_second = jnp.where(odd, main_x, main_c), jnp.where(odd, second_x, second_c)
    right_main, right_second = jnp.where(odd, main_c, main_x), jnp.where(odd, second_c, second_x)
    top = jnp.concatenate([lon_back, left_main, left_second, own_right[:, :, :cut]], axis=2)
    bottom = jnp.concatenate([right_second, own_left, right_main], axis=2)
    return jnp.concatenate([top, bottom], axis=1)


def solution(mesh):
    return jax.shard_map(
        body,
        mesh=mesh,
        in_specs=(P("rep", "lat", "lon", None),) + (P(),) * 14,
        out_specs=P("rep", "lat", "lon", None),
        check_vma=False,
    )
```

```python
import functools
import math
import jax
import jax.numpy as jnp
from jax import lax
from jax.experimental import pallas as pl
from jax.experimental.pallas import tpu as pltpu
from jax.sharding import PartitionSpec as P

HEAD_DIM = 64
LEVELS = 3
WIN_ROWS = 6
WIN_COLS = 12
HALF_ROWS = WIN_ROWS // 2
HALF_COLS = WIN_COLS // 2
TOKENS = LEVELS * WIN_ROWS * WIN_COLS
LANES = 128
AT_ONCE = 5
SCALE = HEAD_DIM**-0.5 * math.log2(math.e)
PARAMS = pltpu.CompilerParams(vmem_limit_bytes=18 * 1024 * 1024)


def norm(wide, gain):
    center = jnp.mean(wide, axis=-1, keepdims=True)
    moved = wide - center
    spread = jnp.mean(jnp.square(moved), axis=-1, keepdims=True)
    return (moved * lax.rsqrt(spread + 1e-05) * gain).astype(jnp.bfloat16)


def rounded(value):
    return value.astype(jnp.bfloat16).astype(jnp.float32)


def attend(windows, gain, qkv_ref, proj_ref, bias, qkv_s, mix_s):
    width = windows[0].shape[1]
    pair = 2 * HEAD_DIM
    for i, x in enumerate(windows):
        normed = norm(x, gain)
        for third in range(3):
            lanes = slice(third * width, (third + 1) * width)
            part = jnp.dot(normed, qkv_ref[:, lanes], preferred_element_type=jnp.float32)
            qkv_s[i, :, lanes] = part.astype(jnp.bfloat16)
    low = lax.broadcasted_iota(jnp.int32, (TOKENS, pair), 1) < HEAD_DIM
    ones = jnp.ones((TOKENS, pair), jnp.bfloat16)
    zeros = jnp.zeros((TOKENS, pair), jnp.bfloat16)
    steps = [
        (i, j, keep)
        for j in range(width // pair)
        for i in range(len(windows))
        for keep in (low, ~low)
    ]

    def scored(step):
        i, j, keep = step
        q = qkv_s[i, :, j * pair : (j + 1) * pair]
        k = qkv_s[i, :, width + j * pair : width + (j + 1) * pair]
        return lax.dot_general(
            q,
            jnp.where(keep, k, zeros),
            (((1,), (1,)), ((), ())),
            preferred_element_type=jnp.float32,
        )

    first = None
    ahead = scored(steps[0])
    for n, (i, j, keep) in enumerate(steps):
        s = ahead * SCALE
        if n + 1 < len(steps):
            ahead = scored(steps[n + 1])
        if bias is not None:
            s = s + bias
        p = jnp.exp2(s - jnp.max(s, axis=-1, keepdims=True)).astype(jnp.bfloat16)
        v = qkv_s[i, :, 2 * width + j * pair : 2 * width + (j + 1) * pair]
        r = jnp.dot(p, jnp.concatenate([v, ones], axis=1), preferred_element_type=jnp.float32)
        if n % 2 == 0:
            first = r
        else:
            mixed = jnp.where(low, first[:, :pair], r[:, :pair])
            total = jnp.where(low, first[:, pair:], r[:, pair:])
            mix_s[i, :, j * pair : (j + 1) * pair] = (mixed / total).astype(jnp.bfloat16)
    return [
        rounded(x + jnp.dot(mix_s[i], proj_ref[...], preferred_element_type=jnp.float32))
        for i, x in enumerate(windows)
    ]


def row_of(dim):
    t = lax.broadcasted_iota(jnp.int32, (TOKENS, TOKENS), dim)
    group = (t * 43691) >> 19
    return group - WIN_ROWS * ((group * 43691) >> 18)


def make_bias(labels_ref, first_row):
    count = labels_ref.shape[0]
    rows = [row_of(0), row_of(1)]
    marks = [jnp.zeros((TOKENS, TOKENS), jnp.int32) for _ in rows]
    for r in range(WIN_ROWS):
        label = labels_ref[lax.rem(first_row + r + count, count)]
        marks = [jnp.where(row == r, label, mark) for row, mark in zip(rows, marks)]
    return jnp.where(marks[0] == marks[1], 0.0, -1e30)


def strip_of(place, center):
    odd = lax.rem(place, 2) == 1
    is_left = odd if center else jnp.logical_not(odd)
    first_row = WIN_ROWS * place + jnp.where(is_left, HALF_ROWS, -HALF_ROWS)
    return is_left, first_row


def load(win_s, w):
    return jnp.concatenate([win_s[w, c] for c in range(win_s.shape[1])], axis=1)


def store(win_s, w, start, value):
    for c in range(win_s.shape[1]):
        win_s[w, c, start : start + value.shape[0], :] = value[:, c * LANES : (c + 1) * LANES]


def attend_all(win_s, gain_ref, qkv_ref, proj_ref, bias_s, qkv_s, mix_s):
    count = win_s.shape[0]

    def some(start, size):
        windows = [load(win_s, start + i) for i in range(size)]
        done = attend(windows, gain_ref[...], qkv_ref, proj_ref, bias_s[...], qkv_s, mix_s)
        for i in range(size):
            store(win_s, start + i, 0, done[i])

    def step(n, carry):
        some(n * AT_ONCE, AT_ONCE)
        return carry

    lax.fori_loop(0, count // AT_ONCE, step, 0)
    if count % AT_ONCE:
        some(count - count % AT_ONCE, count % AT_ONCE)


def put(win_s, group, start, value):
    at, done = start, 0
    while done < value.shape[0]:
        w, c = divmod(at, WIN_COLS)
        size = min(WIN_COLS - c, value.shape[0] - done)
        store(win_s, w, group * WIN_COLS + c, value[done : done + size])
        at, done = at + size, done + size


def merge_rows(upper, lower, gain, weight):
    levels, cols, wide = upper.shape
    a = upper.reshape(levels * cols, wide)
    b = lower.reshape(levels * cols, wide)
    half = wide // 2
    stacked = jnp.concatenate([a[:, :half], b[:, :half], a[:, half:], b[:, half:]], axis=1)
    out = jnp.dot(norm(stacked, gain), weight, preferred_element_type=jnp.float32)
    return out.astype(jnp.bfloat16).astype(jnp.float32).reshape(levels, cols, wide)


def wide(ref, index):
    return ref[index].astype(jnp.float32)


def first_kernel(center, half, lats, place_ref, labels_ref, x_ref, lon_ref, one_ref, two_ref, *refs):
    gain_ref, qkv_ref, proj_ref, mgain_ref, mweight_ref, out_ref, upper_ref, lower_ref = refs[:8]
    win_s, qkv_s, mix_s, bias_s = refs[8:]
    place = place_ref[0]
    is_left, first_row = strip_of(place, center)
    at_seam = jnp.logical_or(place == 0, place == lats - 1)
    span = half + WIN_COLS

    def put_halo(group, l, r):
        one = one_ref[l, r].astype(jnp.float32)
        two = two_ref[l, r].astype(jnp.float32)
        if center:
            put(win_s, group, 0, jnp.where(at_seam, two, one))
        else:
            put(win_s, group, 0, one)
            put(win_s, group, one.shape[0], two)

    @pl.when(is_left)
    def _():
        for l in range(LEVELS):
            for r in range(HALF_ROWS):
                own = x_ref[l, HALF_ROWS + r].astype(jnp.float32)
                put(win_s, l * WIN_ROWS + r, 0, own[HALF_COLS : HALF_COLS + span])
                put_halo(l * WIN_ROWS + HALF_ROWS + r, l, r)

    @pl.when(jnp.logical_not(is_left))
    def _():
        for l in range(LEVELS):
            for r in range(HALF_ROWS):
                put_halo(l * WIN_ROWS + r, l, r)
                group = l * WIN_ROWS + HALF_ROWS + r
                own = x_ref[l, r].astype(jnp.float32)[HALF_COLS + half :]
                put(win_s, group, 0, own)
                put(win_s, group, own.shape[0], lon_ref[l, r].astype(jnp.float32))

    bias_s[...] = make_bias(labels_ref, first_row)
    attend_all(win_s, gain_ref, qkv_ref, proj_ref, bias_s, qkv_s, mix_s)

    groups = win_s.shape[1]
    for l in range(LEVELS):
        for r in range(WIN_ROWS):
            base = (l * WIN_ROWS + r) * WIN_COLS
            for parity in range(2):
                for c in range(groups):
                    pieces = []
                    for w in range(win_s.shape[0]):
                        skip = HALF_COLS if w == 0 else 0
                        size = HALF_COLS // 2 if w in (0, win_s.shape[0] - 1) else HALF_COLS
                        pieces.append(win_s[w, c, pl.ds(base + skip + parity, size, stride=2), :])
                    at = (parity * groups + c) * LANES
                    out_ref[r, l, :, at : at + LANES] = jnp.concatenate(pieces, axis=0).astype(
                        jnp.bfloat16
                    )
    upper_ref[0] = out_ref[0]
    lower_ref[1] = out_ref[WIN_ROWS - 1]
    upper_ref[1] = merge_rows(
        wide(out_ref, 1), wide(out_ref, 2), mgain_ref[...], mweight_ref[...]
    ).astype(jnp.bfloat16)
    lower_ref[0] = merge_rows(
        wide(out_ref, 3), wide(out_ref, 4), mgain_ref[...], mweight_ref[...]
    ).astype(jnp.bfloat16)


def spread_add(spread, upper, lower):
    width = spread.shape[-1] // 4
    parts = [spread[..., i * width : (i + 1) * width] for i in range(4)]
    top = upper + jnp.concatenate([parts[0], parts[2]], axis=-1)
    bottom = lower + jnp.concatenate([parts[1], parts[3]], axis=-1)
    return top.astype(jnp.bfloat16), bottom.astype(jnp.bfloat16)


def gathered(value, r):
    rows = []
    for l in range(LEVELS):
        start = (r * LEVELS + l) * WIN_COLS
        pieces = [value[w][start : start + WIN_COLS] for w in range(len(value))]
        rows.append(jnp.concatenate(pieces, axis=0))
    return jnp.stack(rows)


def spread_of(value, sgain_ref, sweight_ref):
    return jnp.dot(norm(value, sgain_ref[...]), sweight_ref[...], preferred_element_type=jnp.float32)


def coarse_kernel(
    first_ref,
    upper_ref,
    lower_ref,
    prev_ref,
    next_ref,
    mgain_ref,
    mweight_ref,
    gain_ref,
    qkv_ref,
    proj_ref,
    sgain_ref,
    sweight_ref,
    out_ref,
    to_prev_ref,
    to_next_ref,
    edge_ref,
    win_s,
    spread_s,
    qkv_s,
    mix_s,
):
    levels, cols, width = first_ref.shape[1:]
    half_rows = (wide(prev_ref, 1), wide(first_ref, 0), wide(first_ref, 5), wide(next_ref, 0))
    outer = merge_rows(
        jnp.concatenate([half_rows[0], half_rows[2]], axis=0),
        jnp.concatenate([half_rows[1], half_rows[3]], axis=0),
        mgain_ref[...],
        mweight_ref[...],
    )
    rows = [
        wide(prev_ref, 0),
        outer[:levels],
        wide(upper_ref, 1),
        wide(lower_ref, 0),
        outer[levels:],
        wide(next_ref, 1),
    ]
    for r in range(WIN_ROWS):
        for l in range(levels):
            for w in range(win_s.shape[0]):
                start = (r * levels + l) * WIN_COLS
                win_s[w, start : start + WIN_COLS, :] = rows[r][l, w * WIN_COLS : (w + 1) * WIN_COLS]
    count = qkv_s.shape[0]

    def step(n, carry):
        windows = [win_s[n * count + i] for i in range(count)]
        done = attend(windows, gain_ref[...], qkv_ref, proj_ref, None, qkv_s, mix_s)
        for i in range(count):
            win_s[n * count + i] = done[i]
        return carry

    lax.fori_loop(0, win_s.shape[0] // count, step, 0)

    for w in range(win_s.shape[0]):
        spread_s[w] = spread_of(win_s[w], sgain_ref, sweight_ref)
    done = [win_s.at[w] for w in range(win_s.shape[0])]
    spread = [spread_s.at[w] for w in range(win_s.shape[0])]
    to_prev_ref[0] = gathered(done, 0).astype(jnp.bfloat16)
    to_next_ref[1] = gathered(done, WIN_ROWS - 1).astype(jnp.bfloat16)
    to_prev_ref[1], out_ref[0] = spread_add(gathered(spread, 1), half_rows[0], half_rows[1])
    out_ref[1], out_ref[2] = spread_add(gathered(spread, 2), wide(first_ref, 1), wide(first_ref, 2))
    out_ref[3], out_ref[4] = spread_add(gathered(spread, 3), wide(first_ref, 3), wide(first_ref, 4))
    out_ref[5], to_next_ref[0] = spread_add(gathered(spread, 4), half_rows[2], half_rows[3])
    take_edge(out_ref, edge_ref)


def take_edge(out_ref, edge_ref):
    for r in range(WIN_ROWS):
        for l in range(LEVELS):
            edge_ref[r, l] = wide(out_ref, (r, l))[-edge_ref.shape[2] :].astype(jnp.bfloat16)


def giver_kernel(
    first_ref, prev_ref, next_ref, sgain_ref, sweight_ref, out_ref, edge_ref
):
    levels, cols, width = first_ref.shape[1:]
    both = jnp.concatenate([wide(prev_ref, 1), wide(next_ref, 0)], axis=0)
    spread = jnp.dot(
        norm(both.reshape(2 * levels * cols, width), sgain_ref[...]),
        sweight_ref[...],
        preferred_element_type=jnp.float32,
    ).reshape(2 * levels, cols, 2 * width)
    out_ref[0] = prev_ref[0]
    out_ref[5] = next_ref[1]
    out_ref[1], out_ref[2] = spread_add(spread[:levels], wide(first_ref, 1), wide(first_ref, 2))
    out_ref[3], out_ref[4] = spread_add(spread[levels:], wide(first_ref, 3), wide(first_ref, 4))
    take_edge(out_ref, edge_ref)


def rest_kernel(
    center, place_ref, labels_ref, joined_ref, gain_ref, qkv_ref, proj_ref, win_ref, qkv_s, mix_s, bias_s
):
    first_row = strip_of(place_ref[0], center)[1]
    width = win_ref.shape[1] * LANES
    for l in range(LEVELS):
        for r in range(WIN_ROWS):
            joined = wide(joined_ref, (r, l))
            for parity in range(2):
                start = (l * WIN_ROWS + r) * WIN_COLS + parity * HALF_COLS
                for w in range(win_ref.shape[0]):
                    begin = w * HALF_COLS + HALF_COLS // 2
                    lanes = slice(parity * width, (parity + 1) * width)
                    store(win_ref, w, start, joined[begin : begin + HALF_COLS, lanes])
    bias_s[...] = make_bias(labels_ref, first_row)
    attend_all(win_ref, gain_ref, qkv_ref, proj_ref, bias_s, qkv_s, mix_s)


def last_kernel(
    center,
    place_ref,
    labels_ref,
    joined_ref,
    edge_ref,
    rest_ref,
    gain_ref,
    qkv_ref,
    proj_ref,
    own_ref,
    main_ref,
    second_ref,
    win_s,
    qkv_s,
    mix_s,
    bias_s,
    row_s,
):
    is_left, first_row = strip_of(place_ref[0], center)
    groups = win_s.shape[1]
    width = groups * LANES
    extra = edge_ref.shape[2]
    for l in range(LEVELS):
        for r in range(WIN_ROWS):
            edge = wide(edge_ref, (r, l))
            joined = wide(joined_ref, (r, l))
            for parity in range(2):
                lanes = slice(parity * width, (parity + 1) * width)
                start = (l * WIN_ROWS + r) * WIN_COLS + parity * HALF_COLS
                store(win_s, 0, start, edge[:, lanes])
                store(win_s, 0, start + extra, joined[: HALF_COLS - extra, lanes])

    bias_s[...] = make_bias(labels_ref, first_row)
    attend_all(win_s, gain_ref, qkv_ref, proj_ref, bias_s, qkv_s, mix_s)

    def natural(l, r):
        base = (l * WIN_ROWS + r) * WIN_COLS
        for w in range(1 + rest_ref.shape[0]):
            tokens = win_s.at[0] if w == 0 else rest_ref.at[w - 1]
            for parity in range(2):
                start = base + parity * HALF_COLS
                for c in range(groups):
                    row_s[c, pl.ds(w * WIN_COLS + parity, HALF_COLS, stride=2), :] = tokens[
                        c, start : start + HALF_COLS, :
                    ]
        return jnp.concatenate([row_s[c] for c in range(groups)], axis=1)

    cut = main_ref.shape[2]

    def finish(own_row, other_row):
        for l in range(LEVELS):
            for r in range(HALF_ROWS):
                own_ref[l, r] = natural(l, own_row + r).astype(jnp.bfloat16)
                other = natural(l, other_row + r)
                main_ref[l, r] = other[:cut].astype(jnp.bfloat16)
                second_ref[l, r] = other[cut:].astype(jnp.bfloat16)

    @pl.when(is_left)
    def _():
        finish(0, HALF_ROWS)

    @pl.when(jnp.logical_not(is_left))
    def _():
        finish(HALF_ROWS, 0)


def fill_half(is_left, refs, store_row):
    own_ref, main_ref, second_ref, lon_ref = refs
    cut = main_ref.shape[2]

    @pl.when(is_left)
    def _():
        for l in range(LEVELS):
            for r in range(HALF_ROWS):
                pieces = [ref[l, r].astype(jnp.float32) for ref in (second_ref, own_ref, main_ref)]
                store_row(l, r, HALF_ROWS, jnp.concatenate(pieces, axis=0).astype(jnp.bfloat16))

    @pl.when(jnp.logical_not(is_left))
    def _():
        for l in range(LEVELS):
            for r in range(HALF_ROWS):
                pieces = [ref[l, r].astype(jnp.float32) for ref in (lon_ref, main_ref, second_ref)]
                pieces.append(own_ref[l, r].astype(jnp.float32)[:cut])
                store_row(l, r, 0, jnp.concatenate(pieces, axis=0).astype(jnp.bfloat16))


def half_kernel(place_ref, *refs):
    out_ref = refs[-1]

    def store_row(l, r, base, value):
        out_ref[l, r] = value

    fill_half(strip_of(place_ref[0], True)[0], refs[:-1], store_row)


def whole_kernel(place_ref, other_ref, *refs):
    out_ref = refs[-1]

    def store_row(l, r, base, value):
        out_ref[l, base + r] = value
        out_ref[l, HALF_ROWS - base + r] = other_ref[l, r]

    fill_half(strip_of(place_ref[0], False)[0], refs[:-1], store_row)


def load_kernel(*refs):
    count = len(refs) // 2
    sems = refs[-1]
    copies = [
        pltpu.make_async_copy(refs[i], refs[count + i], sems.at[i]) for i in range(count)
    ]
    for copy in copies:
        copy.start()
    for copy in copies:
        copy.wait()


def bf16(*shape):
    return jax.ShapeDtypeStruct(shape, jnp.bfloat16)


def lasting(micros):
    return pl.CostEstimate(flops=0, bytes_accessed=int(micros * 3.69e6), transcendentals=0)


SMEM = pl.BlockSpec(memory_space=pltpu.SMEM)
VMEM = pl.BlockSpec(memory_space=pltpu.VMEM)
ANY = pl.BlockSpec(memory_space=pl.ANY)


def call_load(*arrays):
    return pl.pallas_call(
        load_kernel,
        out_shape=[jax.ShapeDtypeStruct(value.shape, value.dtype) for value in arrays],
        in_specs=[ANY] * len(arrays),
        out_specs=[ANY] * len(arrays),
        scratch_shapes=[pltpu.SemaphoreType.DMA((len(arrays),))],
        cost_estimate=lasting(2),
        compiler_params=PARAMS,
    )(*arrays)


def call_first(center, half, place, labels, x, lon, one, two, weights):
    width = x.shape[-1]
    cols = half // 2
    count = half // WIN_COLS + 1
    paired = (LEVELS, cols, 2 * width)
    return pl.pallas_call(
        functools.partial(first_kernel, center, half, lax.axis_size("lat")),
        out_shape=(bf16(WIN_ROWS, *paired), bf16(2, *paired), bf16(2, *paired)),
        in_specs=[SMEM, SMEM] + [VMEM] * (4 + len(weights)),
        out_specs=(VMEM, VMEM, VMEM),
        scratch_shapes=[
            pltpu.VMEM((count, width // LANES, TOKENS, LANES), jnp.float32),
            pltpu.VMEM((AT_ONCE, TOKENS, 3 * width), jnp.bfloat16),
            pltpu.VMEM((AT_ONCE, TOKENS, width), jnp.bfloat16),
            pltpu.VMEM((TOKENS, TOKENS), jnp.float32),
        ],
        cost_estimate=lasting(10),
        compiler_params=PARAMS,
    )(place, labels, x, lon, one, two, *weights)


def call_coarse(*args):
    rows, levels, cols, width = args[0].shape
    count = cols // WIN_COLS
    paired = (levels, cols, width)
    return pl.pallas_call(
        coarse_kernel,
        out_shape=(
            bf16(rows, *paired),
            bf16(2, *paired),
            bf16(2, *paired),
            bf16(rows, levels, HALF_COLS // 2, width),
        ),
        in_specs=[VMEM] * 12,
        out_specs=(VMEM,) * 4,
        scratch_shapes=[
            pltpu.VMEM((count, TOKENS, width), jnp.float32),
            pltpu.VMEM((count, TOKENS, 2 * width), jnp.float32),
            pltpu.VMEM((math.gcd(count, 2), TOKENS, 3 * width), jnp.bfloat16),
            pltpu.VMEM((math.gcd(count, 2), TOKENS, width), jnp.bfloat16),
        ],
        cost_estimate=lasting(10),
        compiler_params=PARAMS,
    )(*args)


def call_giver(first, prev, following, sgain, sweight):
    rows, levels, cols, width = first.shape
    return pl.pallas_call(
        giver_kernel,
        out_shape=(bf16(*first.shape), bf16(rows, levels, HALF_COLS // 2, width)),
        in_specs=[VMEM] * 5,
        out_specs=(VMEM,) * 2,
        cost_estimate=lasting(1),
        compiler_params=PARAMS,
    )(first, prev, following, sgain, sweight)


def block_scratch(count, width):
    size = min(count, AT_ONCE)
    return [
        pltpu.VMEM((size, TOKENS, 3 * width), jnp.bfloat16),
        pltpu.VMEM((size, TOKENS, width), jnp.bfloat16),
        pltpu.VMEM((TOKENS, TOKENS), jnp.float32),
    ]


def call_rest(center, place, labels, joined, gain, qkv, proj):
    width = joined.shape[3] // 2
    count = 2 * joined.shape[2] // WIN_COLS - 1
    return pl.pallas_call(
        functools.partial(rest_kernel, center),
        out_shape=jax.ShapeDtypeStruct((count, width // LANES, TOKENS, LANES), jnp.float32),
        in_specs=[SMEM, SMEM] + [VMEM] * 4,
        out_specs=VMEM,
        scratch_shapes=block_scratch(count, width),
        cost_estimate=lasting(4 if center else 0.1),
        compiler_params=PARAMS,
    )(place, labels, joined, gain, qkv, proj)


def call_last(center, place, labels, joined, edge, rest, gain, qkv, proj):
    rows, levels, cols, wide_width = joined.shape
    width = wide_width // 2
    half = 2 * cols
    return pl.pallas_call(
        functools.partial(last_kernel, center),
        out_shape=(
            bf16(levels, HALF_ROWS, half, width),
            bf16(levels, HALF_ROWS, half - HALF_COLS, width),
            bf16(levels, HALF_ROWS, HALF_COLS, width),
        ),
        in_specs=[SMEM, SMEM] + [VMEM] * 6,
        out_specs=(VMEM,) * 3,
        scratch_shapes=[pltpu.VMEM((1, width // LANES, TOKENS, LANES), jnp.float32)]
        + block_scratch(1, width)
        + [pltpu.VMEM((width // LANES, half, LANES), jnp.float32)],
        cost_estimate=lasting(3 if center else 0.1),
        compiler_params=PARAMS,
    )(place, labels, joined, edge, rest, gain, qkv, proj)


def call_half(place, own, main, second, lon):
    levels, rows, half, width = own.shape
    return pl.pallas_call(
        half_kernel,
        out_shape=bf16(levels, rows, 2 * half, width),
        in_specs=[SMEM] + [VMEM] * 4,
        out_specs=VMEM,
        cost_estimate=lasting(8),
        compiler_params=PARAMS,
    )(place, own, main, second, lon)


def call_whole(place, other, own, main, second, lon):
    levels, rows, half, width = own.shape
    return pl.pallas_call(
        whole_kernel,
        out_shape=bf16(levels, 2 * rows, 2 * half, width),
        in_specs=[SMEM] + [VMEM] * 5,
        out_specs=VMEM,
        cost_estimate=lasting(2),
        compiler_params=PARAMS,
    )(place, other, own, main, second, lon)


def send(value, move, among=lambda lat, lats: True):
    lats, lons = lax.axis_size("lat"), lax.axis_size("lon")
    pairs = []
    for lat in range(lats):
        for lon in range(lons):
            up, over = move(lat % 2 == 1)
            target = ((lat + up) % lats) * lons + (lon + over) % lons
            if among(lat, lats):
                pairs.append((lat * lons + lon, target))
    return lax.ppermute(value, ("lat", "lon"), pairs)


def body(
    latent,
    band_labels,
    gain_first,
    qkv_first,
    proj_first,
    merge_gain,
    merge_weight,
    gain_coarse,
    qkv_coarse,
    proj_coarse,
    split_gain,
    split_weight,
    gain_last,
    qkv_last,
    proj_last,
):
    place = lax.axis_index("lat")
    odd = place % 2 == 1
    place = place.reshape(1).astype(jnp.int32)
    cols = latent.shape[2]
    half = cols // 2
    edge = HALF_COLS + half
    cut = cols - edge
    flat = lambda gain: gain.reshape(1, -1)

    to_giver = lambda is_odd: (1, 0) if is_odd else (-1, 0)
    to_center = lambda is_odd: (-1, 0) if is_odd else (1, 0)
    extra = HALF_COLS + WIN_COLS
    for_prev = latent[:, :HALF_ROWS]
    for_next = latent[:, HALF_ROWS:]
    lon = send(latent[:, :, :extra], lambda is_odd: (0, -1))
    x_main = send(
        jnp.where(odd, for_prev[:, :, HALF_COLS : HALF_COLS + cut], for_next[:, :, edge:]), to_center
    )
    x_second = send(
        jnp.where(odd, for_prev[:, :, HALF_COLS + cut : edge + WIN_COLS], for_next[:, :, :extra]),
        lambda is_odd: (-1, 0) if is_odd else (1, -1),
    )
    for_giver = jnp.where(
        odd,
        jnp.concatenate([for_next[:, :, edge:], lon[:, HALF_ROWS:]], axis=2),
        for_prev[:, :, HALF_COLS : edge + WIN_COLS],
    )
    c_inner = send(for_giver, to_giver, lambda lat, lats: lat not in (0, lats - 1))
    lon, near, qkv_near = lax.optimization_barrier((lon, latent, qkv_first))
    near, qkv_near = call_load(near, qkv_near)
    x_main, x_second, for_giver, near, qkv_near = lax.optimization_barrier(
        (x_main, x_second, for_giver, near, qkv_near)
    )
    c_seam = send(for_giver, to_giver, lambda lat, lats: lat in (0, lats - 1))

    weights = (flat(gain_first), qkv_near, proj_first, flat(merge_gain), merge_weight)
    first_x, upper_x, lower_x = call_first(
        False, half, place, band_labels, near, lon, x_main, x_second, weights
    )
    from_next = send(upper_x, lambda is_odd: (-1, 0))
    from_prev = send(lower_x, lambda is_odd: (1, 0))
    first_c, upper_c, lower_c = call_first(
        True, half, place, band_labels, near, lon, c_inner, c_seam, weights
    )
    joined_c, to_prev, to_next, edge_c = call_coarse(
        first_c,
        upper_c,
        lower_c,
        from_prev,
        from_next,
        flat(merge_gain),
        merge_weight,
        flat(gain_coarse),
        qkv_coarse,
        proj_coarse,
        flat(split_gain),
        split_weight,
    )
    back_next = send(to_prev, lambda is_odd: (-1, 0))
    back_prev = send(to_next, lambda is_odd: (1, 0))
    edge_c = send(edge_c, lambda is_odd: (1, 0) if is_odd else (-1, 1))
    weights = (flat(gain_last), qkv_last, proj_last)
    rest_c = call_rest(True, place, band_labels, joined_c, *weights)
    rest_c, first_x = lax.optimization_barrier((rest_c, first_x))
    joined_x, edge_x = call_giver(first_x, back_prev, back_next, flat(split_gain), split_weight)
    rest_c, joined_x = lax.optimization_barrier((rest_c, joined_x))
    edge_x = send(edge_x, lambda is_odd: (-1, 1) if is_odd else (1, 0))
    own_c, main_c, second_c = call_last(True, place, band_labels, joined_c, edge_c, rest_c, *weights)
    own_c, joined_x = lax.optimization_barrier((own_c, joined_x))
    second_c = send(second_c, lambda is_odd: (1, 0) if is_odd else (-1, 1))
    lon_c = send(own_c[:, :, cut:], lambda is_odd: (0, 1), lambda lat, lats: lat % 2 == 0)
    main_c = send(main_c, to_giver)
    rest_x = call_rest(False, place, band_labels, joined_x, *weights)
    edge_x, second_c, lon_c = lax.optimization_barrier((edge_x, second_c, lon_c))
    own_x, main_x, second_x = call_last(False, place, band_labels, joined_x, edge_x, rest_x, *weights)
    main_x = send(main_x, to_center)
    second_x = send(second_x, lambda is_odd: (-1, 1) if is_odd else (1, 0))
    lon_x = send(own_x[:, :, cut:], lambda is_odd: (0, 1), lambda lat, lats: lat % 2 == 1)
    lower = call_half(place, own_c, main_c, second_c, lon_c)
    return call_whole(place, lower, own_x, main_x, second_x, lon_x)


def solution(mesh):
    return jax.shard_map(
        body,
        mesh=mesh,
        in_specs=(P("rep", "lat", "lon", None),) + (P(),) * 14,
        out_specs=P("rep", "lat", "lon", None),
        check_vma=False,
    )
```

```python
import functools
import math
import jax
import jax.numpy as jnp
from jax import lax
from jax.experimental import pallas as pl
from jax.experimental.pallas import tpu as pltpu
from jax.sharding import PartitionSpec as P

HEAD_DIM = 64
LEVELS = 3
WIN_ROWS = 6
WIN_COLS = 12
HALF_ROWS = WIN_ROWS // 2
HALF_COLS = WIN_COLS // 2
TOKENS = LEVELS * WIN_ROWS * WIN_COLS
LANES = 128
AT_ONCE = 5
SCALE = HEAD_DIM**-0.5 * math.log2(math.e)
PARAMS = pltpu.CompilerParams(vmem_limit_bytes=18 * 1024 * 1024)


def norm(wide, gain):
    center = jnp.mean(wide, axis=-1, keepdims=True)
    moved = wide - center
    spread = jnp.mean(jnp.square(moved), axis=-1, keepdims=True)
    return (moved * lax.rsqrt(spread + 1e-05) * gain).astype(jnp.bfloat16)


def rounded(value):
    return value.astype(jnp.bfloat16).astype(jnp.float32)


def attend(windows, gain, qkv_ref, proj_ref, bias, qkv_s, mix_s):
    width = windows[0].shape[1]
    pair = 2 * HEAD_DIM
    for i, x in enumerate(windows):
        normed = norm(x, gain)
        for third in range(3):
            lanes = slice(third * width, (third + 1) * width)
            part = jnp.dot(normed, qkv_ref[:, lanes], preferred_element_type=jnp.float32)
            qkv_s[i, :, lanes] = part.astype(jnp.bfloat16)
    low = lax.broadcasted_iota(jnp.int32, (TOKENS, pair), 1) < HEAD_DIM
    ones = jnp.ones((TOKENS, pair), jnp.bfloat16)
    zeros = jnp.zeros((TOKENS, pair), jnp.bfloat16)
    steps = [
        (i, j, keep)
        for j in range(width // pair)
        for i in range(len(windows))
        for keep in (low, ~low)
    ]

    def scored(step):
        i, j, keep = step
        q = qkv_s[i, :, j * pair : (j + 1) * pair]
        k = qkv_s[i, :, width + j * pair : width + (j + 1) * pair]
        return lax.dot_general(
            q,
            jnp.where(keep, k, zeros),
            (((1,), (1,)), ((), ())),
            preferred_element_type=jnp.float32,
        )

    first = None
    ahead = scored(steps[0])
    for n, (i, j, keep) in enumerate(steps):
        s = ahead * SCALE
        if n + 1 < len(steps):
            ahead = scored(steps[n + 1])
        if bias is not None:
            s = s + bias
        p = jnp.exp2(s - jnp.max(s, axis=-1, keepdims=True)).astype(jnp.bfloat16)
        v = qkv_s[i, :, 2 * width + j * pair : 2 * width + (j + 1) * pair]
        r = jnp.dot(p, jnp.concatenate([v, ones], axis=1), preferred_element_type=jnp.float32)
        if n % 2 == 0:
            first = r
        else:
            mixed = jnp.where(low, first[:, :pair], r[:, :pair])
            total = jnp.where(low, first[:, pair:], r[:, pair:])
            mix_s[i, :, j * pair : (j + 1) * pair] = (mixed / total).astype(jnp.bfloat16)
    return [
        rounded(x + jnp.dot(mix_s[i], proj_ref[...], preferred_element_type=jnp.float32))
        for i, x in enumerate(windows)
    ]


def row_of(dim):
    t = lax.broadcasted_iota(jnp.int32, (TOKENS, TOKENS), dim)
    group = (t * 43691) >> 19
    return group - WIN_ROWS * ((group * 43691) >> 18)


def make_bias(labels_ref, first_row):
    count = labels_ref.shape[0]
    rows = [row_of(0), row_of(1)]
    marks = [jnp.zeros((TOKENS, TOKENS), jnp.int32) for _ in rows]
    for r in range(WIN_ROWS):
        label = labels_ref[lax.rem(first_row + r + count, count)]
        marks = [jnp.where(row == r, label, mark) for row, mark in zip(rows, marks)]
    return jnp.where(marks[0] == marks[1], 0.0, -1e30)


def strip_of(place, center):
    odd = lax.rem(place, 2) == 1
    is_left = odd if center else jnp.logical_not(odd)
    first_row = WIN_ROWS * place + jnp.where(is_left, HALF_ROWS, -HALF_ROWS)
    return is_left, first_row


def load(win_s, w):
    return jnp.concatenate([win_s[w, c] for c in range(win_s.shape[1])], axis=1)


def store(win_s, w, start, value):
    for c in range(win_s.shape[1]):
        win_s[w, c, start : start + value.shape[0], :] = value[:, c * LANES : (c + 1) * LANES]


def attend_all(win_s, gain_ref, qkv_ref, proj_ref, bias_s, qkv_s, mix_s):
    count = win_s.shape[0]

    def some(start, size):
        windows = [load(win_s, start + i) for i in range(size)]
        done = attend(windows, gain_ref[...], qkv_ref, proj_ref, bias_s[...], qkv_s, mix_s)
        for i in range(size):
            store(win_s, start + i, 0, done[i])

    def step(n, carry):
        some(n * AT_ONCE, AT_ONCE)
        return carry

    lax.fori_loop(0, count // AT_ONCE, step, 0)
    if count % AT_ONCE:
        some(count - count % AT_ONCE, count % AT_ONCE)


def put(win_s, group, start, value):
    at, done = start, 0
    while done < value.shape[0]:
        w, c = divmod(at, WIN_COLS)
        size = min(WIN_COLS - c, value.shape[0] - done)
        store(win_s, w, group * WIN_COLS + c, value[done : done + size])
        at, done = at + size, done + size


def merge_rows(upper, lower, gain, weight):
    levels, cols, wide = upper.shape
    a = upper.reshape(levels * cols, wide)
    b = lower.reshape(levels * cols, wide)
    half = wide // 2
    stacked = jnp.concatenate([a[:, :half], b[:, :half], a[:, half:], b[:, half:]], axis=1)
    out = jnp.dot(norm(stacked, gain), weight, preferred_element_type=jnp.float32)
    return out.astype(jnp.bfloat16).astype(jnp.float32).reshape(levels, cols, wide)


def wide(ref, index):
    return ref[index].astype(jnp.float32)


def first_kernel(center, half, lats, place_ref, labels_ref, x_ref, lon_ref, one_ref, two_ref, *refs):
    gain_ref, qkv_ref, proj_ref, mgain_ref, mweight_ref, out_ref, upper_ref, lower_ref = refs[:8]
    win_s, qkv_s, mix_s, bias_s = refs[8:]
    place = place_ref[0]
    is_left, first_row = strip_of(place, center)
    at_seam = jnp.logical_or(place == 0, place == lats - 1)
    span = half + WIN_COLS

    def put_halo(group, l, r):
        one = one_ref[l, r].astype(jnp.float32)
        two = two_ref[l, r].astype(jnp.float32)
        if center:
            put(win_s, group, 0, jnp.where(at_seam, two, one))
        else:
            put(win_s, group, 0, one)
            put(win_s, group, one.shape[0], two)

    @pl.when(is_left)
    def _():
        for l in range(LEVELS):
            for r in range(HALF_ROWS):
                own = x_ref[l, HALF_ROWS + r].astype(jnp.float32)
                put(win_s, l * WIN_ROWS + r, 0, own[HALF_COLS : HALF_COLS + span])
                put_halo(l * WIN_ROWS + HALF_ROWS + r, l, r)

    @pl.when(jnp.logical_not(is_left))
    def _():
        for l in range(LEVELS):
            for r in range(HALF_ROWS):
                put_halo(l * WIN_ROWS + r, l, r)
                group = l * WIN_ROWS + HALF_ROWS + r
                own = x_ref[l, r].astype(jnp.float32)[HALF_COLS + half :]
                put(win_s, group, 0, own)
                put(win_s, group, own.shape[0], lon_ref[l, r].astype(jnp.float32))

    bias_s[...] = make_bias(labels_ref, first_row)
    attend_all(win_s, gain_ref, qkv_ref, proj_ref, bias_s, qkv_s, mix_s)

    groups = win_s.shape[1]
    for l in range(LEVELS):
        for r in range(WIN_ROWS):
            base = (l * WIN_ROWS + r) * WIN_COLS
            for parity in range(2):
                for c in range(groups):
                    pieces = []
                    for w in range(win_s.shape[0]):
                        skip = HALF_COLS if w == 0 else 0
                        size = HALF_COLS // 2 if w in (0, win_s.shape[0] - 1) else HALF_COLS
                        pieces.append(win_s[w, c, pl.ds(base + skip + parity, size, stride=2), :])
                    at = (parity * groups + c) * LANES
                    out_ref[r, l, :, at : at + LANES] = jnp.concatenate(pieces, axis=0).astype(
                        jnp.bfloat16
                    )
    upper_ref[0] = out_ref[0]
    lower_ref[1] = out_ref[WIN_ROWS - 1]
    upper_ref[1] = merge_rows(
        wide(out_ref, 1), wide(out_ref, 2), mgain_ref[...], mweight_ref[...]
    ).astype(jnp.bfloat16)
    lower_ref[0] = merge_rows(
        wide(out_ref, 3), wide(out_ref, 4), mgain_ref[...], mweight_ref[...]
    ).astype(jnp.bfloat16)


def spread_add(spread, upper, lower):
    width = spread.shape[-1] // 4
    parts = [spread[..., i * width : (i + 1) * width] for i in range(4)]
    top = upper + jnp.concatenate([parts[0], parts[2]], axis=-1)
    bottom = lower + jnp.concatenate([parts[1], parts[3]], axis=-1)
    return top.astype(jnp.bfloat16), bottom.astype(jnp.bfloat16)


def gathered(value, r):
    rows = []
    for l in range(LEVELS):
        start = (r * LEVELS + l) * WIN_COLS
        pieces = [value[w][start : start + WIN_COLS] for w in range(len(value))]
        rows.append(jnp.concatenate(pieces, axis=0))
    return jnp.stack(rows)


def spread_of(value, sgain_ref, sweight_ref):
    return jnp.dot(norm(value, sgain_ref[...]), sweight_ref[...], preferred_element_type=jnp.float32)


def coarse_kernel(
    first_ref,
    upper_ref,
    lower_ref,
    prev_ref,
    next_ref,
    mgain_ref,
    mweight_ref,
    gain_ref,
    qkv_ref,
    proj_ref,
    sgain_ref,
    sweight_ref,
    out_ref,
    to_prev_ref,
    to_next_ref,
    edge_ref,
    win_s,
    spread_s,
    qkv_s,
    mix_s,
):
    levels, cols, width = first_ref.shape[1:]
    half_rows = (wide(prev_ref, 1), wide(first_ref, 0), wide(first_ref, 5), wide(next_ref, 0))
    outer = merge_rows(
        jnp.concatenate([half_rows[0], half_rows[2]], axis=0),
        jnp.concatenate([half_rows[1], half_rows[3]], axis=0),
        mgain_ref[...],
        mweight_ref[...],
    )
    rows = [
        wide(prev_ref, 0),
        outer[:levels],
        wide(upper_ref, 1),
        wide(lower_ref, 0),
        outer[levels:],
        wide(next_ref, 1),
    ]
    for r in range(WIN_ROWS):
        for l in range(levels):
            for w in range(win_s.shape[0]):
                start = (r * levels + l) * WIN_COLS
                win_s[w, start : start + WIN_COLS, :] = rows[r][l, w * WIN_COLS : (w + 1) * WIN_COLS]
    count = qkv_s.shape[0]

    def step(n, carry):
        windows = [win_s[n * count + i] for i in range(count)]
        done = attend(windows, gain_ref[...], qkv_ref, proj_ref, None, qkv_s, mix_s)
        for i in range(count):
            win_s[n * count + i] = done[i]
        return carry

    lax.fori_loop(0, win_s.shape[0] // count, step, 0)

    for w in range(win_s.shape[0]):
        spread_s[w] = spread_of(win_s[w], sgain_ref, sweight_ref)
    done = [win_s.at[w] for w in range(win_s.shape[0])]
    spread = [spread_s.at[w] for w in range(win_s.shape[0])]
    to_prev_ref[0] = gathered(done, 0).astype(jnp.bfloat16)
    to_next_ref[1] = gathered(done, WIN_ROWS - 1).astype(jnp.bfloat16)
    to_prev_ref[1], out_ref[0] = spread_add(gathered(spread, 1), half_rows[0], half_rows[1])
    out_ref[1], out_ref[2] = spread_add(gathered(spread, 2), wide(first_ref, 1), wide(first_ref, 2))
    out_ref[3], out_ref[4] = spread_add(gathered(spread, 3), wide(first_ref, 3), wide(first_ref, 4))
    out_ref[5], to_next_ref[0] = spread_add(gathered(spread, 4), half_rows[2], half_rows[3])
    take_edge(out_ref, edge_ref)


def take_edge(out_ref, edge_ref):
    for r in range(WIN_ROWS):
        for l in range(LEVELS):
            edge_ref[r, l] = wide(out_ref, (r, l))[-edge_ref.shape[2] :].astype(jnp.bfloat16)


def giver_kernel(
    first_ref, prev_ref, next_ref, sgain_ref, sweight_ref, out_ref, edge_ref
):
    levels, cols, width = first_ref.shape[1:]
    both = jnp.concatenate([wide(prev_ref, 1), wide(next_ref, 0)], axis=0)
    spread = jnp.dot(
        norm(both.reshape(2 * levels * cols, width), sgain_ref[...]),
        sweight_ref[...],
        preferred_element_type=jnp.float32,
    ).reshape(2 * levels, cols, 2 * width)
    out_ref[0] = prev_ref[0]
    out_ref[5] = next_ref[1]
    out_ref[1], out_ref[2] = spread_add(spread[:levels], wide(first_ref, 1), wide(first_ref, 2))
    out_ref[3], out_ref[4] = spread_add(spread[levels:], wide(first_ref, 3), wide(first_ref, 4))
    take_edge(out_ref, edge_ref)


def rest_kernel(
    center, place_ref, labels_ref, joined_ref, gain_ref, qkv_ref, proj_ref, win_ref, qkv_s, mix_s, bias_s
):
    first_row = strip_of(place_ref[0], center)[1]
    width = win_ref.shape[1] * LANES
    for l in range(LEVELS):
        for r in range(WIN_ROWS):
            joined = wide(joined_ref, (r, l))
            for parity in range(2):
                start = (l * WIN_ROWS + r) * WIN_COLS + parity * HALF_COLS
                for w in range(win_ref.shape[0]):
                    begin = w * HALF_COLS + HALF_COLS // 2
                    lanes = slice(parity * width, (parity + 1) * width)
                    store(win_ref, w, start, joined[begin : begin + HALF_COLS, lanes])
    bias_s[...] = make_bias(labels_ref, first_row)
    attend_all(win_ref, gain_ref, qkv_ref, proj_ref, bias_s, qkv_s, mix_s)


def last_kernel(
    center,
    place_ref,
    labels_ref,
    joined_ref,
    edge_ref,
    rest_ref,
    gain_ref,
    qkv_ref,
    proj_ref,
    own_ref,
    *refs,
):
    *back_refs, win_s, qkv_s, mix_s, bias_s, row_s = refs
    is_left, first_row = strip_of(place_ref[0], center)
    groups = win_s.shape[1]
    width = groups * LANES
    extra = edge_ref.shape[2]
    for l in range(LEVELS):
        for r in range(WIN_ROWS):
            edge = wide(edge_ref, (r, l))
            joined = wide(joined_ref, (r, l))
            for parity in range(2):
                lanes = slice(parity * width, (parity + 1) * width)
                start = (l * WIN_ROWS + r) * WIN_COLS + parity * HALF_COLS
                store(win_s, 0, start, edge[:, lanes])
                store(win_s, 0, start + extra, joined[: HALF_COLS - extra, lanes])

    bias_s[...] = make_bias(labels_ref, first_row)
    attend_all(win_s, gain_ref, qkv_ref, proj_ref, bias_s, qkv_s, mix_s)

    def natural(l, r):
        base = (l * WIN_ROWS + r) * WIN_COLS
        for w in range(1 + rest_ref.shape[0]):
            tokens = win_s.at[0] if w == 0 else rest_ref.at[w - 1]
            for parity in range(2):
                start = base + parity * HALF_COLS
                for c in range(groups):
                    row_s[c, pl.ds(w * WIN_COLS + parity, HALF_COLS, stride=2), :] = tokens[
                        c, start : start + HALF_COLS, :
                    ]
        return jnp.concatenate([row_s[c] for c in range(groups)], axis=1)

    def finish(own_row, other_row):
        for l in range(LEVELS):
            for r in range(HALF_ROWS):
                own_ref[l, r] = natural(l, own_row + r).astype(jnp.bfloat16)
                other = natural(l, other_row + r)
                at = 0
                for ref in back_refs:
                    ref[l, r] = other[at : at + ref.shape[2]].astype(jnp.bfloat16)
                    at += ref.shape[2]

    @pl.when(is_left)
    def _():
        finish(0, HALF_ROWS)

    @pl.when(jnp.logical_not(is_left))
    def _():
        finish(HALF_ROWS, 0)


def half_kernel(place_ref, own_ref, main_ref, lon_ref, out_ref):
    cut = out_ref.shape[2] - lon_ref.shape[2] - own_ref.shape[2]

    def fill(middle_ref, right_ref):
        for l in range(LEVELS):
            for r in range(HALF_ROWS):
                pieces = [ref[l, r].astype(jnp.float32) for ref in (lon_ref, middle_ref)]
                pieces.append(right_ref[l, r].astype(jnp.float32)[:cut])
                out_ref[l, r] = jnp.concatenate(pieces, axis=0).astype(jnp.bfloat16)

    is_left = strip_of(place_ref[0], True)[0]

    @pl.when(is_left)
    def _():
        fill(own_ref, main_ref)

    @pl.when(jnp.logical_not(is_left))
    def _():
        fill(main_ref, own_ref)


def load_kernel(*refs):
    count = len(refs) // 2
    sems = refs[-1]
    copies = [
        pltpu.make_async_copy(refs[i], refs[count + i], sems.at[i]) for i in range(count)
    ]
    for copy in copies:
        copy.start()
    for copy in copies:
        copy.wait()


def bf16(*shape):
    return jax.ShapeDtypeStruct(shape, jnp.bfloat16)


def lasting(micros):
    return pl.CostEstimate(flops=0, bytes_accessed=int(micros * 3.69e6), transcendentals=0)


SMEM = pl.BlockSpec(memory_space=pltpu.SMEM)
VMEM = pl.BlockSpec(memory_space=pltpu.VMEM)
ANY = pl.BlockSpec(memory_space=pl.ANY)


def call_load(*arrays):
    return pl.pallas_call(
        load_kernel,
        out_shape=[jax.ShapeDtypeStruct(value.shape, value.dtype) for value in arrays],
        in_specs=[ANY] * len(arrays),
        out_specs=[ANY] * len(arrays),
        scratch_shapes=[pltpu.SemaphoreType.DMA((len(arrays),))],
        cost_estimate=lasting(2),
        compiler_params=PARAMS,
    )(*arrays)


def call_first(center, half, place, labels, x, lon, one, two, weights):
    width = x.shape[-1]
    cols = half // 2
    count = half // WIN_COLS + 1
    paired = (LEVELS, cols, 2 * width)
    return pl.pallas_call(
        functools.partial(first_kernel, center, half, lax.axis_size("lat")),
        out_shape=(bf16(WIN_ROWS, *paired), bf16(2, *paired), bf16(2, *paired)),
        in_specs=[SMEM, SMEM] + [VMEM] * (4 + len(weights)),
        out_specs=(VMEM, VMEM, VMEM),
        scratch_shapes=[
            pltpu.VMEM((count, width // LANES, TOKENS, LANES), jnp.float32),
            pltpu.VMEM((AT_ONCE, TOKENS, 3 * width), jnp.bfloat16),
            pltpu.VMEM((AT_ONCE, TOKENS, width), jnp.bfloat16),
            pltpu.VMEM((TOKENS, TOKENS), jnp.float32),
        ],
        cost_estimate=lasting(10),
        compiler_params=PARAMS,
    )(place, labels, x, lon, one, two, *weights)


def call_coarse(*args):
    rows, levels, cols, width = args[0].shape
    count = cols // WIN_COLS
    paired = (levels, cols, width)
    return pl.pallas_call(
        coarse_kernel,
        out_shape=(
            bf16(rows, *paired),
            bf16(2, *paired),
            bf16(2, *paired),
            bf16(rows, levels, HALF_COLS // 2, width),
        ),
        in_specs=[VMEM] * 12,
        out_specs=(VMEM,) * 4,
        scratch_shapes=[
            pltpu.VMEM((count, TOKENS, width), jnp.float32),
            pltpu.VMEM((count, TOKENS, 2 * width), jnp.float32),
            pltpu.VMEM((math.gcd(count, 2), TOKENS, 3 * width), jnp.bfloat16),
            pltpu.VMEM((math.gcd(count, 2), TOKENS, width), jnp.bfloat16),
        ],
        cost_estimate=lasting(10),
        compiler_params=PARAMS,
    )(*args)


def call_giver(first, prev, following, sgain, sweight):
    rows, levels, cols, width = first.shape
    return pl.pallas_call(
        giver_kernel,
        out_shape=(bf16(*first.shape), bf16(rows, levels, HALF_COLS // 2, width)),
        in_specs=[VMEM] * 5,
        out_specs=(VMEM,) * 2,
        cost_estimate=lasting(1),
        compiler_params=PARAMS,
    )(first, prev, following, sgain, sweight)


def block_scratch(count, width):
    size = min(count, AT_ONCE)
    return [
        pltpu.VMEM((size, TOKENS, 3 * width), jnp.bfloat16),
        pltpu.VMEM((size, TOKENS, width), jnp.bfloat16),
        pltpu.VMEM((TOKENS, TOKENS), jnp.float32),
    ]


def call_rest(center, place, labels, joined, gain, qkv, proj):
    width = joined.shape[3] // 2
    count = 2 * joined.shape[2] // WIN_COLS - 1
    return pl.pallas_call(
        functools.partial(rest_kernel, center),
        out_shape=jax.ShapeDtypeStruct((count, width // LANES, TOKENS, LANES), jnp.float32),
        in_specs=[SMEM, SMEM] + [VMEM] * 4,
        out_specs=VMEM,
        scratch_shapes=block_scratch(count, width),
        cost_estimate=lasting(4 if center else 0.1),
        compiler_params=PARAMS,
    )(place, labels, joined, gain, qkv, proj)


def call_last(center, place, labels, joined, edge, rest, gain, qkv, proj):
    rows, levels, cols, wide_width = joined.shape
    width = wide_width // 2
    half = 2 * cols
    sizes = (half, half) if center else (half, half - HALF_COLS, HALF_COLS)
    return pl.pallas_call(
        functools.partial(last_kernel, center),
        out_shape=tuple(bf16(levels, HALF_ROWS, size, width) for size in sizes),
        in_specs=[SMEM, SMEM] + [VMEM] * 6,
        out_specs=(VMEM,) * len(sizes),
        scratch_shapes=[pltpu.VMEM((1, width // LANES, TOKENS, LANES), jnp.float32)]
        + block_scratch(1, width)
        + [pltpu.VMEM((width // LANES, half, LANES), jnp.float32)],
        cost_estimate=lasting(3 if center else 0.1),
        compiler_params=PARAMS,
    )(place, labels, joined, edge, rest, gain, qkv, proj)


def call_half(place, own, main, lon):
    levels, rows, half, width = own.shape
    return pl.pallas_call(
        half_kernel,
        out_shape=bf16(levels, rows, 2 * half, width),
        in_specs=[SMEM] + [VMEM] * 3,
        out_specs=VMEM,
        cost_estimate=lasting(8),
        compiler_params=PARAMS,
    )(place, own, main, lon)


def send(value, move, among=lambda lat, lats: True):
    lats, lons = lax.axis_size("lat"), lax.axis_size("lon")
    pairs = []
    for lat in range(lats):
        for lon in range(lons):
            up, over = move(lat % 2 == 1)
            target = ((lat + up) % lats) * lons + (lon + over) % lons
            if among(lat, lats):
                pairs.append((lat * lons + lon, target))
    return lax.ppermute(value, ("lat", "lon"), pairs)


def body(
    latent,
    band_labels,
    gain_first,
    qkv_first,
    proj_first,
    merge_gain,
    merge_weight,
    gain_coarse,
    qkv_coarse,
    proj_coarse,
    split_gain,
    split_weight,
    gain_last,
    qkv_last,
    proj_last,
):
    place = lax.axis_index("lat")
    odd = place % 2 == 1
    place = place.reshape(1).astype(jnp.int32)
    cols = latent.shape[2]
    half = cols // 2
    edge = HALF_COLS + half
    cut = cols - edge
    flat = lambda gain: gain.reshape(1, -1)

    to_giver = lambda is_odd: (1, 0) if is_odd else (-1, 0)
    to_center = lambda is_odd: (-1, 0) if is_odd else (1, 0)
    extra = HALF_COLS + WIN_COLS
    for_prev = latent[:, :HALF_ROWS]
    for_next = latent[:, HALF_ROWS:]
    lon = send(latent[:, :, :extra], lambda is_odd: (0, -1))
    x_main = send(
        jnp.where(odd, for_prev[:, :, HALF_COLS : HALF_COLS + cut], for_next[:, :, edge:]), to_center
    )
    x_second = send(
        jnp.where(odd, for_prev[:, :, HALF_COLS + cut : edge + WIN_COLS], for_next[:, :, :extra]),
        lambda is_odd: (-1, 0) if is_odd else (1, -1),
    )
    for_giver = jnp.where(
        odd,
        jnp.concatenate([for_next[:, :, edge:], lon[:, HALF_ROWS:]], axis=2),
        for_prev[:, :, HALF_COLS : edge + WIN_COLS],
    )
    c_inner = send(for_giver, to_giver, lambda lat, lats: lat not in (0, lats - 1))
    lon, near, qkv_near = lax.optimization_barrier((lon, latent, qkv_first))
    near, qkv_near = call_load(near, qkv_near)
    x_main, x_second, for_giver, near, qkv_near = lax.optimization_barrier(
        (x_main, x_second, for_giver, near, qkv_near)
    )
    c_seam = send(for_giver, to_giver, lambda lat, lats: lat in (0, lats - 1))

    weights = (flat(gain_first), qkv_near, proj_first, flat(merge_gain), merge_weight)
    first_x, upper_x, lower_x = call_first(
        False, half, place, band_labels, near, lon, x_main, x_second, weights
    )
    from_next = send(upper_x, lambda is_odd: (-1, 0))
    from_prev = send(lower_x, lambda is_odd: (1, 0))
    first_c, upper_c, lower_c = call_first(
        True, half, place, band_labels, near, lon, c_inner, c_seam, weights
    )
    joined_c, to_prev, to_next, edge_c = call_coarse(
        first_c,
        upper_c,
        lower_c,
        from_prev,
        from_next,
        flat(merge_gain),
        merge_weight,
        flat(gain_coarse),
        qkv_coarse,
        proj_coarse,
        flat(split_gain),
        split_weight,
    )
    back_next = send(to_prev, lambda is_odd: (-1, 0))
    back_prev = send(to_next, lambda is_odd: (1, 0))
    edge_c = send(edge_c, lambda is_odd: (1, 0) if is_odd else (-1, 1))
    weights = (flat(gain_last), qkv_last, proj_last)
    rest_c = call_rest(True, place, band_labels, joined_c, *weights)
    rest_c, first_x = lax.optimization_barrier((rest_c, first_x))
    joined_x, edge_x = call_giver(first_x, back_prev, back_next, flat(split_gain), split_weight)
    rest_c, joined_x = lax.optimization_barrier((rest_c, joined_x))
    edge_x = send(edge_x, lambda is_odd: (-1, 1) if is_odd else (1, 0))
    own_c, main_c = call_last(True, place, band_labels, joined_c, edge_c, rest_c, *weights)
    own_c, joined_x = lax.optimization_barrier((own_c, joined_x))
    edge_x, main_c = lax.optimization_barrier((edge_x, main_c))
    main_c = send(main_c, to_giver)
    rest_x = call_rest(False, place, band_labels, joined_x, *weights)
    own_x, main_x, second_x = call_last(False, place, band_labels, joined_x, edge_x, rest_x, *weights)
    main_x = send(main_x, to_center)
    second_x = send(second_x, lambda is_odd: (-1, 1) if is_odd else (1, 0))
    lon_x = send(own_x[:, :, cut:], lambda is_odd: (0, 1), lambda lat, lats: lat % 2 == 1)
    lon_c = send(jnp.where(odd, main_c[:, :, cut:], own_c[:, :, cut:]), lambda is_odd: (0, 1))
    lower = call_half(place, own_c, main_c, lon_c)
    bottom = jnp.concatenate([second_x, own_x, main_x], axis=2)
    top = jnp.concatenate([lon_x, main_x, second_x, own_x[:, :, :cut]], axis=2)
    first_rows, last_rows = jnp.where(odd, top, lower), jnp.where(odd, lower, bottom)
    return jnp.concatenate([first_rows, last_rows], axis=1)


def solution(mesh):
    return jax.shard_map(
        body,
        mesh=mesh,
        in_specs=(P("rep", "lat", "lon", None),) + (P(),) * 14,
        out_specs=P("rep", "lat", "lon", None),
        check_vma=False,
    )
```

```python
import functools
import math
import jax
import jax.numpy as jnp
from jax import lax
from jax.experimental import pallas as pl
from jax.experimental.pallas import tpu as pltpu
from jax.sharding import PartitionSpec as P

HEAD_DIM = 64
LEVELS = 3
WIN_ROWS = 6
WIN_COLS = 12
HALF_ROWS = WIN_ROWS // 2
HALF_COLS = WIN_COLS // 2
TOKENS = LEVELS * WIN_ROWS * WIN_COLS
LANES = 128
SCALE = HEAD_DIM**-0.5 * math.log2(math.e)
PARAMS = pltpu.CompilerParams(vmem_limit_bytes=18 * 1024 * 1024)


def norm(wide, gain):
    center = jnp.mean(wide, axis=-1, keepdims=True)
    moved = wide - center
    spread = jnp.mean(jnp.square(moved), axis=-1, keepdims=True)
    return (moved * lax.rsqrt(spread + 1e-05) * gain).astype(jnp.bfloat16)


def rounded(value):
    return value.astype(jnp.bfloat16).astype(jnp.float32)


def attend(windows, gain, qkv_ref, proj_ref, bias, qkv_s, mix_s):
    width = windows[0].shape[1]
    pair = 2 * HEAD_DIM
    for i, x in enumerate(windows):
        normed = norm(x, gain)
        for third in range(3):
            lanes = slice(third * width, (third + 1) * width)
            part = jnp.dot(normed, qkv_ref[:, lanes], preferred_element_type=jnp.float32)
            qkv_s[i, :, lanes] = part.astype(jnp.bfloat16)
    low = lax.broadcasted_iota(jnp.int32, (TOKENS, pair), 1) < HEAD_DIM
    ones = jnp.ones((TOKENS, pair), jnp.bfloat16)
    zeros = jnp.zeros((TOKENS, pair), jnp.bfloat16)
    steps = [
        (i, j, keep)
        for j in range(width // pair)
        for i in range(len(windows))
        for keep in (low, ~low)
    ]

    def scored(step):
        i, j, keep = step
        q = qkv_s[i, :, j * pair : (j + 1) * pair]
        k = qkv_s[i, :, width + j * pair : width + (j + 1) * pair]
        return lax.dot_general(
            q,
            jnp.where(keep, k, zeros),
            (((1,), (1,)), ((), ())),
            preferred_element_type=jnp.float32,
        )

    first = None
    ahead = scored(steps[0])
    for n, (i, j, keep) in enumerate(steps):
        s = ahead * SCALE
        if n + 1 < len(steps):
            ahead = scored(steps[n + 1])
        if bias is not None:
            s = s + bias
        p = jnp.exp2(s - jnp.max(s, axis=-1, keepdims=True)).astype(jnp.bfloat16)
        v = qkv_s[i, :, 2 * width + j * pair : 2 * width + (j + 1) * pair]
        r = jnp.dot(p, jnp.concatenate([v, ones], axis=1), preferred_element_type=jnp.float32)
        if n % 2 == 0:
            first = r
        else:
            mixed = jnp.where(low, first[:, :pair], r[:, :pair])
            total = jnp.where(low, first[:, pair:], r[:, pair:])
            mix_s[i, :, j * pair : (j + 1) * pair] = (mixed / total).astype(jnp.bfloat16)
    return [
        rounded(x + jnp.dot(mix_s[i], proj_ref[...], preferred_element_type=jnp.float32))
        for i, x in enumerate(windows)
    ]


def row_of(dim):
    t = lax.broadcasted_iota(jnp.int32, (TOKENS, TOKENS), dim)
    group = (t * 43691) >> 19
    return group - WIN_ROWS * ((group * 43691) >> 18)


def make_bias(labels_ref, first_row):
    count = labels_ref.shape[0]
    rows = [row_of(0), row_of(1)]
    marks = [jnp.zeros((TOKENS, TOKENS), jnp.int32) for _ in rows]
    for r in range(WIN_ROWS):
        label = labels_ref[lax.rem(first_row + r + count, count)]
        marks = [jnp.where(row == r, label, mark) for row, mark in zip(rows, marks)]
    return jnp.where(marks[0] == marks[1], 0.0, -1e30)


def strip_of(place, center):
    odd = lax.rem(place, 2) == 1
    is_left = odd if center else jnp.logical_not(odd)
    first_row = WIN_ROWS * place + jnp.where(is_left, HALF_ROWS, -HALF_ROWS)
    return is_left, first_row


def load(win_s, w):
    return jnp.concatenate([win_s[w, c] for c in range(win_s.shape[1])], axis=1)


def store(win_s, w, start, value):
    for c in range(win_s.shape[1]):
        win_s[w, c, start : start + value.shape[0], :] = value[:, c * LANES : (c + 1) * LANES]


def attend_all(win_s, gain_ref, qkv_ref, proj_ref, bias_s, qkv_s, mix_s):
    count, at_once = win_s.shape[0], qkv_s.shape[0]

    def some(start, size):
        windows = [load(win_s, start + i) for i in range(size)]
        done = attend(windows, gain_ref[...], qkv_ref, proj_ref, bias_s[...], qkv_s, mix_s)
        for i in range(size):
            store(win_s, start + i, 0, done[i])

    def step(n, carry):
        some(n * at_once, at_once)
        return carry

    lax.fori_loop(0, count // at_once, step, 0)
    if count % at_once:
        some(count - count % at_once, count % at_once)


def put(win_s, group, start, value):
    at, done = start, 0
    while done < value.shape[0]:
        w, c = divmod(at, WIN_COLS)
        size = min(WIN_COLS - c, value.shape[0] - done)
        store(win_s, w, group * WIN_COLS + c, value[done : done + size])
        at, done = at + size, done + size


def merge_rows(upper, lower, gain, weight):
    levels, cols, wide = upper.shape
    a = upper.reshape(levels * cols, wide)
    b = lower.reshape(levels * cols, wide)
    half = wide // 2
    stacked = jnp.concatenate([a[:, :half], b[:, :half], a[:, half:], b[:, half:]], axis=1)
    out = jnp.dot(norm(stacked, gain), weight, preferred_element_type=jnp.float32)
    return out.astype(jnp.bfloat16).astype(jnp.float32).reshape(levels, cols, wide)


def wide(ref, index):
    return ref[index].astype(jnp.float32)


def first_kernel(center, half, lats, place_ref, labels_ref, x_ref, lon_ref, one_ref, two_ref, *refs):
    gain_ref, qkv_ref, proj_ref, mgain_ref, mweight_ref, out_ref, upper_ref, lower_ref = refs[:8]
    win_s, qkv_s, mix_s, bias_s = refs[8:]
    place = place_ref[0]
    is_left, first_row = strip_of(place, center)
    at_seam = jnp.logical_or(place == 0, place == lats - 1)
    span = half + WIN_COLS

    def put_halo(group, l, r):
        one = one_ref[l, r].astype(jnp.float32)
        two = two_ref[l, r].astype(jnp.float32)
        if center:
            put(win_s, group, 0, jnp.where(at_seam, two, one))
        else:
            put(win_s, group, 0, one)
            put(win_s, group, one.shape[0], two)

    @pl.when(is_left)
    def _():
        for l in range(LEVELS):
            for r in range(HALF_ROWS):
                own = x_ref[l, HALF_ROWS + r].astype(jnp.float32)
                put(win_s, l * WIN_ROWS + r, 0, own[HALF_COLS : HALF_COLS + span])
                put_halo(l * WIN_ROWS + HALF_ROWS + r, l, r)

    @pl.when(jnp.logical_not(is_left))
    def _():
        for l in range(LEVELS):
            for r in range(HALF_ROWS):
                put_halo(l * WIN_ROWS + r, l, r)
                group = l * WIN_ROWS + HALF_ROWS + r
                own = x_ref[l, r].astype(jnp.float32)[HALF_COLS + half :]
                put(win_s, group, 0, own)
                put(win_s, group, own.shape[0], lon_ref[l, r].astype(jnp.float32))

    bias_s[...] = make_bias(labels_ref, first_row)
    attend_all(win_s, gain_ref, qkv_ref, proj_ref, bias_s, qkv_s, mix_s)

    groups = win_s.shape[1]
    for l in range(LEVELS):
        for r in range(WIN_ROWS):
            base = (l * WIN_ROWS + r) * WIN_COLS
            for parity in range(2):
                for c in range(groups):
                    pieces = []
                    for w in range(win_s.shape[0]):
                        skip = HALF_COLS if w == 0 else 0
                        size = HALF_COLS // 2 if w in (0, win_s.shape[0] - 1) else HALF_COLS
                        pieces.append(win_s[w, c, pl.ds(base + skip + parity, size, stride=2), :])
                    at = (parity * groups + c) * LANES
                    out_ref[r, l, :, at : at + LANES] = jnp.concatenate(pieces, axis=0).astype(
                        jnp.bfloat16
                    )
    upper_ref[0] = out_ref[0]
    lower_ref[1] = out_ref[WIN_ROWS - 1]
    upper_ref[1] = merge_rows(
        wide(out_ref, 1), wide(out_ref, 2), mgain_ref[...], mweight_ref[...]
    ).astype(jnp.bfloat16)
    lower_ref[0] = merge_rows(
        wide(out_ref, 3), wide(out_ref, 4), mgain_ref[...], mweight_ref[...]
    ).astype(jnp.bfloat16)


def spread_add(spread, upper, lower):
    width = spread.shape[-1] // 4
    parts = [spread[..., i * width : (i + 1) * width] for i in range(4)]
    top = upper + jnp.concatenate([parts[0], parts[2]], axis=-1)
    bottom = lower + jnp.concatenate([parts[1], parts[3]], axis=-1)
    return top.astype(jnp.bfloat16), bottom.astype(jnp.bfloat16)


def gathered(value, r):
    rows = []
    for l in range(LEVELS):
        start = (r * LEVELS + l) * WIN_COLS
        pieces = [value[w][start : start + WIN_COLS] for w in range(len(value))]
        rows.append(jnp.concatenate(pieces, axis=0))
    return jnp.stack(rows)


def spread_of(value, sgain_ref, sweight_ref):
    return jnp.dot(norm(value, sgain_ref[...]), sweight_ref[...], preferred_element_type=jnp.float32)


def coarse_kernel(
    first_ref,
    upper_ref,
    lower_ref,
    prev_ref,
    next_ref,
    mgain_ref,
    mweight_ref,
    gain_ref,
    qkv_ref,
    proj_ref,
    sgain_ref,
    sweight_ref,
    out_ref,
    to_prev_ref,
    to_next_ref,
    edge_ref,
    win_s,
    spread_s,
    qkv_s,
    mix_s,
):
    levels, cols, width = first_ref.shape[1:]
    half_rows = (wide(prev_ref, 1), wide(first_ref, 0), wide(first_ref, 5), wide(next_ref, 0))
    outer = merge_rows(
        jnp.concatenate([half_rows[0], half_rows[2]], axis=0),
        jnp.concatenate([half_rows[1], half_rows[3]], axis=0),
        mgain_ref[...],
        mweight_ref[...],
    )
    rows = [
        wide(prev_ref, 0),
        outer[:levels],
        wide(upper_ref, 1),
        wide(lower_ref, 0),
        outer[levels:],
        wide(next_ref, 1),
    ]
    for r in range(WIN_ROWS):
        for l in range(levels):
            for w in range(win_s.shape[0]):
                start = (r * levels + l) * WIN_COLS
                win_s[w, start : start + WIN_COLS, :] = rows[r][l, w * WIN_COLS : (w + 1) * WIN_COLS]
    count = qkv_s.shape[0]

    def step(n, carry):
        windows = [win_s[n * count + i] for i in range(count)]
        done = attend(windows, gain_ref[...], qkv_ref, proj_ref, None, qkv_s, mix_s)
        for i in range(count):
            win_s[n * count + i] = done[i]
        return carry

    lax.fori_loop(0, win_s.shape[0] // count, step, 0)

    for w in range(win_s.shape[0]):
        spread_s[w] = spread_of(win_s[w], sgain_ref, sweight_ref)
    done = [win_s.at[w] for w in range(win_s.shape[0])]
    spread = [spread_s.at[w] for w in range(win_s.shape[0])]
    to_prev_ref[0] = gathered(done, 0).astype(jnp.bfloat16)
    to_next_ref[1] = gathered(done, WIN_ROWS - 1).astype(jnp.bfloat16)
    to_prev_ref[1], out_ref[0] = spread_add(gathered(spread, 1), half_rows[0], half_rows[1])
    out_ref[1], out_ref[2] = spread_add(gathered(spread, 2), wide(first_ref, 1), wide(first_ref, 2))
    out_ref[3], out_ref[4] = spread_add(gathered(spread, 3), wide(first_ref, 3), wide(first_ref, 4))
    out_ref[5], to_next_ref[0] = spread_add(gathered(spread, 4), half_rows[2], half_rows[3])
    take_edge(out_ref, edge_ref)


def take_edge(out_ref, edge_ref):
    for r in range(WIN_ROWS):
        for l in range(LEVELS):
            edge_ref[r, l] = wide(out_ref, (r, l))[-edge_ref.shape[2] :].astype(jnp.bfloat16)


def giver_kernel(
    first_ref, prev_ref, next_ref, sgain_ref, sweight_ref, out_ref, edge_ref
):
    levels, cols, width = first_ref.shape[1:]
    both = jnp.concatenate([wide(prev_ref, 1), wide(next_ref, 0)], axis=0)
    spread = jnp.dot(
        norm(both.reshape(2 * levels * cols, width), sgain_ref[...]),
        sweight_ref[...],
        preferred_element_type=jnp.float32,
    ).reshape(2 * levels, cols, 2 * width)
    out_ref[0] = prev_ref[0]
    out_ref[5] = next_ref[1]
    out_ref[1], out_ref[2] = spread_add(spread[:levels], wide(first_ref, 1), wide(first_ref, 2))
    out_ref[3], out_ref[4] = spread_add(spread[levels:], wide(first_ref, 3), wide(first_ref, 4))
    take_edge(out_ref, edge_ref)


def rest_kernel(
    center, place_ref, labels_ref, joined_ref, gain_ref, qkv_ref, proj_ref, win_ref, qkv_s, mix_s, bias_s
):
    first_row = strip_of(place_ref[0], center)[1]
    width = win_ref.shape[1] * LANES
    for l in range(LEVELS):
        for r in range(WIN_ROWS):
            joined = wide(joined_ref, (r, l))
            for parity in range(2):
                start = (l * WIN_ROWS + r) * WIN_COLS + parity * HALF_COLS
                for w in range(win_ref.shape[0]):
                    begin = w * HALF_COLS + HALF_COLS // 2
                    lanes = slice(parity * width, (parity + 1) * width)
                    store(win_ref, w, start, joined[begin : begin + HALF_COLS, lanes])
    bias_s[...] = make_bias(labels_ref, first_row)
    attend_all(win_ref, gain_ref, qkv_ref, proj_ref, bias_s, qkv_s, mix_s)


def last_kernel(
    center,
    place_ref,
    labels_ref,
    joined_ref,
    edge_ref,
    rest_ref,
    gain_ref,
    qkv_ref,
    proj_ref,
    own_ref,
    *refs,
):
    *back_refs, win_s, qkv_s, mix_s, bias_s, row_s = refs
    is_left, first_row = strip_of(place_ref[0], center)
    groups = win_s.shape[1]
    width = groups * LANES
    extra = edge_ref.shape[2]
    for l in range(LEVELS):
        for r in range(WIN_ROWS):
            edge = wide(edge_ref, (r, l))
            joined = wide(joined_ref, (r, l))
            for parity in range(2):
                lanes = slice(parity * width, (parity + 1) * width)
                start = (l * WIN_ROWS + r) * WIN_COLS + parity * HALF_COLS
                store(win_s, 0, start, edge[:, lanes])
                store(win_s, 0, start + extra, joined[: HALF_COLS - extra, lanes])

    bias_s[...] = make_bias(labels_ref, first_row)
    attend_all(win_s, gain_ref, qkv_ref, proj_ref, bias_s, qkv_s, mix_s)

    def natural(l, r):
        base = (l * WIN_ROWS + r) * WIN_COLS
        for w in range(1 + rest_ref.shape[0]):
            tokens = win_s.at[0] if w == 0 else rest_ref.at[w - 1]
            for parity in range(2):
                start = base + parity * HALF_COLS
                for c in range(groups):
                    row_s[c, pl.ds(w * WIN_COLS + parity, HALF_COLS, stride=2), :] = tokens[
                        c, start : start + HALF_COLS, :
                    ]
        return jnp.concatenate([row_s[c] for c in range(groups)], axis=1)

    def finish(own_row, other_row):
        for l in range(LEVELS):
            for r in range(HALF_ROWS):
                own_ref[l, r] = natural(l, own_row + r).astype(jnp.bfloat16)
                other = natural(l, other_row + r)
                at = 0
                for ref in back_refs:
                    ref[l, r] = other[at : at + ref.shape[2]].astype(jnp.bfloat16)
                    at += ref.shape[2]

    @pl.when(is_left)
    def _():
        finish(0, HALF_ROWS)

    @pl.when(jnp.logical_not(is_left))
    def _():
        finish(HALF_ROWS, 0)


def half_kernel(place_ref, own_ref, main_ref, lon_ref, out_ref):
    cut = out_ref.shape[2] - lon_ref.shape[2] - own_ref.shape[2]

    def fill(middle_ref, right_ref):
        for l in range(LEVELS):
            for r in range(HALF_ROWS):
                pieces = [ref[l, r].astype(jnp.float32) for ref in (lon_ref, middle_ref)]
                pieces.append(right_ref[l, r].astype(jnp.float32)[:cut])
                out_ref[l, r] = jnp.concatenate(pieces, axis=0).astype(jnp.bfloat16)

    is_left = strip_of(place_ref[0], True)[0]

    @pl.when(is_left)
    def _():
        fill(own_ref, main_ref)

    @pl.when(jnp.logical_not(is_left))
    def _():
        fill(main_ref, own_ref)


def load_kernel(*refs):
    count = len(refs) // 2
    sems = refs[-1]
    copies = [
        pltpu.make_async_copy(refs[i], refs[count + i], sems.at[i]) for i in range(count)
    ]
    for copy in copies:
        copy.start()
    for copy in copies:
        copy.wait()


def bf16(*shape):
    return jax.ShapeDtypeStruct(shape, jnp.bfloat16)


def lasting(micros):
    return pl.CostEstimate(flops=0, bytes_accessed=int(micros * 3.69e6), transcendentals=0)


SMEM = pl.BlockSpec(memory_space=pltpu.SMEM)
VMEM = pl.BlockSpec(memory_space=pltpu.VMEM)
ANY = pl.BlockSpec(memory_space=pl.ANY)


def call_load(*arrays):
    return pl.pallas_call(
        load_kernel,
        out_shape=[jax.ShapeDtypeStruct(value.shape, value.dtype) for value in arrays],
        in_specs=[ANY] * len(arrays),
        out_specs=[ANY] * len(arrays),
        scratch_shapes=[pltpu.SemaphoreType.DMA((len(arrays),))],
        cost_estimate=lasting(2),
        compiler_params=PARAMS,
    )(*arrays)


def call_first(center, half, place, labels, x, lon, one, two, weights):
    width = x.shape[-1]
    cols = half // 2
    count = half // WIN_COLS + 1
    paired = (LEVELS, cols, 2 * width)
    return pl.pallas_call(
        functools.partial(first_kernel, center, half, lax.axis_size("lat")),
        out_shape=(bf16(WIN_ROWS, *paired), bf16(2, *paired), bf16(2, *paired)),
        in_specs=[SMEM, SMEM] + [VMEM] * (4 + len(weights)),
        out_specs=(VMEM, VMEM, VMEM),
        scratch_shapes=[
            pltpu.VMEM((count, width // LANES, TOKENS, LANES), jnp.float32),
        ]
        + block_scratch(count if center else 2, width),
        cost_estimate=lasting(10),
        compiler_params=PARAMS,
    )(place, labels, x, lon, one, two, *weights)


def call_coarse(*args):
    rows, levels, cols, width = args[0].shape
    count = cols // WIN_COLS
    paired = (levels, cols, width)
    return pl.pallas_call(
        coarse_kernel,
        out_shape=(
            bf16(rows, *paired),
            bf16(2, *paired),
            bf16(2, *paired),
            bf16(rows, levels, HALF_COLS // 2, width),
        ),
        in_specs=[VMEM] * 12,
        out_specs=(VMEM,) * 4,
        scratch_shapes=[
            pltpu.VMEM((count, TOKENS, width), jnp.float32),
            pltpu.VMEM((count, TOKENS, 2 * width), jnp.float32),
            pltpu.VMEM((math.gcd(count, 2), TOKENS, 3 * width), jnp.bfloat16),
            pltpu.VMEM((math.gcd(count, 2), TOKENS, width), jnp.bfloat16),
        ],
        cost_estimate=lasting(10),
        compiler_params=PARAMS,
    )(*args)


def call_giver(first, prev, following, sgain, sweight):
    rows, levels, cols, width = first.shape
    return pl.pallas_call(
        giver_kernel,
        out_shape=(bf16(*first.shape), bf16(rows, levels, HALF_COLS // 2, width)),
        in_specs=[VMEM] * 5,
        out_specs=(VMEM,) * 2,
        cost_estimate=lasting(1),
        compiler_params=PARAMS,
    )(first, prev, following, sgain, sweight)


def block_scratch(size, width):
    return [
        pltpu.VMEM((size, TOKENS, 3 * width), jnp.bfloat16),
        pltpu.VMEM((size, TOKENS, width), jnp.bfloat16),
        pltpu.VMEM((TOKENS, TOKENS), jnp.float32),
    ]


def call_rest(center, place, labels, joined, gain, qkv, proj):
    width = joined.shape[3] // 2
    count = 2 * joined.shape[2] // WIN_COLS - 1
    return pl.pallas_call(
        functools.partial(rest_kernel, center),
        out_shape=jax.ShapeDtypeStruct((count, width // LANES, TOKENS, LANES), jnp.float32),
        in_specs=[SMEM, SMEM] + [VMEM] * 4,
        out_specs=VMEM,
        scratch_shapes=block_scratch(1, width),
        cost_estimate=lasting(4 if center else 0.1),
        compiler_params=PARAMS,
    )(place, labels, joined, gain, qkv, proj)


def call_last(center, place, labels, joined, edge, rest, gain, qkv, proj):
    rows, levels, cols, wide_width = joined.shape
    width = wide_width // 2
    half = 2 * cols
    sizes = (half, half) if center else (half, half - HALF_COLS, HALF_COLS)
    return pl.pallas_call(
        functools.partial(last_kernel, center),
        out_shape=tuple(bf16(levels, HALF_ROWS, size, width) for size in sizes),
        in_specs=[SMEM, SMEM] + [VMEM] * 6,
        out_specs=(VMEM,) * len(sizes),
        scratch_shapes=[pltpu.VMEM((1, width // LANES, TOKENS, LANES), jnp.float32)]
        + block_scratch(1, width)
        + [pltpu.VMEM((width // LANES, half, LANES), jnp.float32)],
        cost_estimate=lasting(3 if center else 0.1),
        compiler_params=PARAMS,
    )(place, labels, joined, edge, rest, gain, qkv, proj)


def call_half(place, own, main, lon):
    levels, rows, half, width = own.shape
    return pl.pallas_call(
        half_kernel,
        out_shape=bf16(levels, rows, 2 * half, width),
        in_specs=[SMEM] + [VMEM] * 3,
        out_specs=VMEM,
        cost_estimate=lasting(8),
        compiler_params=PARAMS,
    )(place, own, main, lon)


def send(value, move, among=lambda lat, lats: True):
    lats, lons = lax.axis_size("lat"), lax.axis_size("lon")
    pairs = []
    for lat in range(lats):
        for lon in range(lons):
            up, over = move(lat % 2 == 1)
            target = ((lat + up) % lats) * lons + (lon + over) % lons
            if among(lat, lats):
                pairs.append((lat * lons + lon, target))
    return lax.ppermute(value, ("lat", "lon"), pairs)


def body(
    latent,
    band_labels,
    gain_first,
    qkv_first,
    proj_first,
    merge_gain,
    merge_weight,
    gain_coarse,
    qkv_coarse,
    proj_coarse,
    split_gain,
    split_weight,
    gain_last,
    qkv_last,
    proj_last,
):
    place = lax.axis_index("lat")
    odd = place % 2 == 1
    place = place.reshape(1).astype(jnp.int32)
    cols = latent.shape[2]
    half = cols // 2
    edge = HALF_COLS + half
    cut = cols - edge
    flat = lambda gain: gain.reshape(1, -1)

    to_giver = lambda is_odd: (1, 0) if is_odd else (-1, 0)
    to_center = lambda is_odd: (-1, 0) if is_odd else (1, 0)
    extra = HALF_COLS + WIN_COLS
    for_prev = latent[:, :HALF_ROWS]
    for_next = latent[:, HALF_ROWS:]
    lon = send(latent[:, :, :extra], lambda is_odd: (0, -1))
    x_main = send(
        jnp.where(odd, for_prev[:, :, HALF_COLS : HALF_COLS + cut], for_next[:, :, edge:]), to_center
    )
    x_second = send(
        jnp.where(odd, for_prev[:, :, HALF_COLS + cut : edge + WIN_COLS], for_next[:, :, :extra]),
        lambda is_odd: (-1, 0) if is_odd else (1, -1),
    )
    for_giver = jnp.where(
        odd,
        jnp.concatenate([for_next[:, :, edge:], lon[:, HALF_ROWS:]], axis=2),
        for_prev[:, :, HALF_COLS : edge + WIN_COLS],
    )
    c_inner = send(for_giver, to_giver, lambda lat, lats: lat not in (0, lats - 1))
    lon, near, qkv_near = lax.optimization_barrier((lon, latent, qkv_first))
    near, qkv_near = call_load(near, qkv_near)
    x_main, x_second, for_giver, near, qkv_near = lax.optimization_barrier(
        (x_main, x_second, for_giver, near, qkv_near)
    )
    c_seam = send(for_giver, to_giver, lambda lat, lats: lat in (0, lats - 1))

    weights = (flat(gain_first), qkv_near, proj_first, flat(merge_gain), merge_weight)
    first_x, upper_x, lower_x = call_first(
        False, half, place, band_labels, near, lon, x_main, x_second, weights
    )
    from_next = send(upper_x, lambda is_odd: (-1, 0))
    from_prev = send(lower_x, lambda is_odd: (1, 0))
    first_c, upper_c, lower_c = call_first(
        True, half, place, band_labels, near, lon, c_inner, c_seam, weights
    )
    joined_c, to_prev, to_next, edge_c = call_coarse(
        first_c,
        upper_c,
        lower_c,
        from_prev,
        from_next,
        flat(merge_gain),
        merge_weight,
        flat(gain_coarse),
        qkv_coarse,
        proj_coarse,
        flat(split_gain),
        split_weight,
    )
    back_next = send(to_prev, lambda is_odd: (-1, 0))
    back_prev = send(to_next, lambda is_odd: (1, 0))
    edge_c = send(edge_c, lambda is_odd: (1, 0) if is_odd else (-1, 1))
    weights = (flat(gain_last), qkv_last, proj_last)
    rest_c = call_rest(True, place, band_labels, joined_c, *weights)
    rest_c, first_x = lax.optimization_barrier((rest_c, first_x))
    joined_x, edge_x = call_giver(first_x, back_prev, back_next, flat(split_gain), split_weight)
    rest_c, joined_x = lax.optimization_barrier((rest_c, joined_x))
    edge_x = send(edge_x, lambda is_odd: (-1, 1) if is_odd else (1, 0))
    own_c, main_c = call_last(True, place, band_labels, joined_c, edge_c, rest_c, *weights)
    own_c, joined_x = lax.optimization_barrier((own_c, joined_x))
    edge_x, main_c = lax.optimization_barrier((edge_x, main_c))
    main_c = send(main_c, to_giver)
    rest_x = call_rest(False, place, band_labels, joined_x, *weights)
    own_x, main_x, second_x = call_last(False, place, band_labels, joined_x, edge_x, rest_x, *weights)
    main_x = send(main_x, to_center)
    second_x = send(second_x, lambda is_odd: (-1, 1) if is_odd else (1, 0))
    lon_x = send(own_x[:, :, cut:], lambda is_odd: (0, 1), lambda lat, lats: lat % 2 == 1)
    lon_c = send(jnp.where(odd, main_c[:, :, cut:], own_c[:, :, cut:]), lambda is_odd: (0, 1))
    lower = call_half(place, own_c, main_c, lon_c)
    bottom = jnp.concatenate([second_x, own_x, main_x], axis=2)
    top = jnp.concatenate([lon_x, main_x, second_x, own_x[:, :, :cut]], axis=2)
    first_rows, last_rows = jnp.where(odd, top, lower), jnp.where(odd, lower, bottom)
    return jnp.concatenate([first_rows, last_rows], axis=1)


def solution(mesh):
    return jax.shard_map(
        body,
        mesh=mesh,
        in_specs=(P("rep", "lat", "lon", None),) + (P(),) * 14,
        out_specs=P("rep", "lat", "lon", None),
        check_vma=False,
    )
```
